256 devices in a mesh: inst: 32 (over y, z_hi, x), tp: 8 (over z_lo, core).
Axes of the slice: x: 4, y: 4, z: 8 (z_hi: 2, z_lo: 4; z = z_hi * 4 + z_lo), core: 2. Of those that a mesh axis runs over, the one named last changes fastest.
Arguments:
- new_queries: bfloat16 [512, 2, 8192], P(('inst', 'tp')), may hold values from -6 to 6
- new_keys: bfloat16 [512, 2, 1024], P(('inst', 'tp')), may hold values from -6 to 6
- new_values: bfloat16 [512, 2, 1024], P(('inst', 'tp')), may hold values from -6 to 6
- key_pool: bfloat16 [2048, 128, 1024], P('inst', None, 'tp'), may hold values from -6 to 6
- value_pool: bfloat16 [2048, 128, 1024], P('inst', None, 'tp'), may hold values from -6 to 6
- lengths: int32 [512], replicated, may hold values from 1 to 512
- page_table: int32 [512, 4], P('inst'), may hold values from 0 to 63, as said below
- mig_row: int32 [352], replicated, may hold values from 0 to 511, as said below
- mig_source: int32 [352], replicated, may hold values from 0 to 31, as said below
- mig_pages: int32 [352, 4], replicated, may hold values from 0 to 63, as said below
Outputs:
- attention: bfloat16 [512, 2, 8192], P(('inst', 'tp'))
- key_moved: bfloat16 [2048, 128, 1024], P('inst', None, 'tp')
- value_moved: bfloat16 [2048, 128, 1024], P('inst', None, 'tp')
The draws below stay inside these ranges and needn't reach their ends.
Inputs may be any that keep to these rules, and one draw needn't show every extreme that they name: `page_table`: the 4 pages of the 16 rows of one instance are its 64 pool pages, each once. `mig_row`: the rows are distinct; every instance is the target of exactly 11 migrations. `mig_source`: every instance is the source of exactly 11 migrations, to distinct instances, never to itself. `mig_pages`: the pages of the migrations leaving one instance are distinct.
All inputs are finite; a program needn't handle non-finite values.
Results may differ from the reference program's by a relative error of at most 0.0049.
Values may be sent and summed in bfloat16 or wider, within the bound.
No kernel may reach another device: no remote copies, remote signals or barrier semaphores. Data moves between devices by JAX's collectives and lax.ppermute only.
A program may use at most 128 MiB of HBM per device.

```python
import math
import jax
import jax.numpy as jnp
from jax import lax

HQ = 64
KVH = 8
HD = 128
PAGE = 128
MAXP = 4
ROWS = 16
POOL = 64
MOVES = 11
MIGS = 352
N_INST = 32


def permutations(key, count, width):

    def one_order(sub_key):
        return jax.random.permutation(sub_key, width)
    return jax.vmap(one_order)(jax.random.split(key, count)).astype(jnp.int32)


def migration_plan(key):
    order = jax.random.permutation(jax.random.fold_in(key, 101), N_INST).astype(jnp.int32)
    places = jnp.arange(N_INST, dtype=jnp.int32)
    step_index = jnp.arange(MOVES, dtype=jnp.int32)
    target_place = (places[None, :] + 1 + step_index[:, None]) % N_INST
    targets = order[target_place]
    sources = jnp.broadcast_to(order[None, :], (MOVES, N_INST))
    slot_orders = permutations(jax.random.fold_in(key, 102), N_INST, ROWS)
    slots = slot_orders[targets, jnp.broadcast_to(step_index[:, None], (MOVES, N_INST))]
    rows = targets * ROWS + slots
    return (sources.reshape(-1).astype(jnp.int32), rows.reshape(-1).astype(jnp.int32))


def drawn_heads(key):
    rows_pick = jax.random.randint(jax.random.fold_in(key, 201), (N_INST,), 0, ROWS) + jnp.arange(N_INST, dtype=jnp.int32) * ROWS
    kv_head = jax.random.randint(jax.random.fold_in(key, 202), (N_INST,), 0, KVH)
    member = jax.random.randint(jax.random.fold_in(key, 203), (N_INST,), 0, HQ // KVH)
    signs = (jax.random.randint(jax.random.fold_in(key, 204), (N_INST, HD), 0, 2) * 2 - 1).astype(jnp.float32)
    strength = 4.0 + (jnp.arange(N_INST, dtype=jnp.int32) % 3).astype(jnp.float32)
    return (rows_pick, kv_head, member, signs, strength)


def base_floats(key, shape):
    return jnp.clip(jax.random.normal(key, shape, jnp.float32), -6.0, 6.0)


def draw_new_queries(key, part):
    rows_pick, kv_head, member, signs, strength = drawn_heads(key)
    key = jax.random.fold_in(key, 11)
    shape = (N_INST * ROWS, 2, HQ * HD)
    base = base_floats(key, shape)
    head = kv_head * (HQ // KVH) + member
    columns = head[:, None] * HD + jnp.arange(HD, dtype=jnp.int32)[None, :]
    return base.at[rows_pick[:, None], 1, columns].set(strength[:, None] * signs).astype(jnp.bfloat16)


def draw_new_keys(key, part):
    rows_pick, kv_head, member, signs, strength = drawn_heads(key)
    key = jax.random.fold_in(key, 12)
    shape = (N_INST * ROWS, 2, KVH * HD)
    base = base_floats(key, shape)
    columns = kv_head[:, None] * HD + jnp.arange(HD, dtype=jnp.int32)[None, :]
    lowered = (jnp.arange(HD, dtype=jnp.int32) < max(1, HD // 32)).astype(jnp.float32)
    first_key = 6.0 * signs
    second_key = signs * (6.0 - lowered[None, :])
    base = base.at[rows_pick[:, None], 0, columns].set(first_key)
    return base.at[rows_pick[:, None], 1, columns].set(second_key).astype(jnp.bfloat16)


def draw_mig_row(key, part):
    sources, rows = migration_plan(key)
    return rows


def draw_mig_source(key, part):
    sources, rows = migration_plan(key)
    return sources


def draw_lengths(key, part):
    sources, rows = migration_plan(key)
    key = jax.random.fold_in(key, 5)
    base = jax.random.randint(key, (N_INST * ROWS,), 1, MAXP * PAGE + 1)
    longer = MAXP * PAGE - jax.random.randint(jax.random.fold_in(key, 6), (MIGS,), 0, PAGE // 2)
    longer = longer.at[0].set(MAXP * PAGE)
    return base.at[rows].set(longer).astype(jnp.int32)


def draw_page_table(key, part):
    key = jax.random.fold_in(key, 7)
    return permutations(key, N_INST, POOL).reshape(N_INST * ROWS, MAXP)


def draw_mig_pages(key, part):
    sources, rows = migration_plan(key)
    key = jax.random.fold_in(key, 8)
    orders = permutations(key, N_INST, POOL)
    which = jnp.arange(MIGS, dtype=jnp.int32) // N_INST
    columns = which[:, None] * MAXP + jnp.arange(MAXP, dtype=jnp.int32)[None, :]
    return orders[sources[:, None], columns].astype(jnp.int32)


def levels(stream_key, extent, cuts, smallest, top_value):
    gain, own = 1.0, jax.random.fold_in(stream_key, 6)
    for axis_at, shards_of in cuts:
        draws = jnp.exp(jax.random.uniform(jax.random.fold_in(own, axis_at), (shards_of,), jnp.float32, smallest / len(cuts), top_value / len(cuts)))
        gain = gain * jnp.repeat(draws, extent[axis_at] // shards_of).reshape([-1 if axis == axis_at else 1 for axis in range(len(extent))])
    return gain


def gaussian(stream_key, dims, scale, reach, cuts=(), kind=jnp.bfloat16):
    values = jax.random.normal(stream_key, dims, jnp.float32) * scale
    if len(cuts) > 0:
        values = levels(stream_key, dims, cuts, -0.22, 0.18) * values
    return jnp.clip(values, min=-reach, max=reach).astype(kind)


def setup_inputs(seed: int = 0) -> dict:
    key_list = jax.random.split(jax.random.key(seed), 11)
    new_queries = draw_new_queries(jax.random.fold_in(key_list[10], 71), 0)
    new_keys = draw_new_keys(jax.random.fold_in(key_list[10], 71), 0)
    new_values = gaussian(key_list[2], (N_INST * ROWS, 2, KVH * HD), 1.0, 6.0, ((0, 256),))
    key_pool = gaussian(key_list[3], (N_INST * POOL, PAGE, KVH * HD), 1.0, 6.0, ((0, 32), (2, 8)))
    value_pool = gaussian(key_list[4], (N_INST * POOL, PAGE, KVH * HD), 1.0, 6.0, ((0, 32), (2, 8)))
    lengths = draw_lengths(jax.random.fold_in(key_list[10], 71), 0)
    page_table = draw_page_table(jax.random.fold_in(key_list[10], 71), 0)
    mig_row = draw_mig_row(jax.random.fold_in(key_list[10], 71), 0)
    mig_source = draw_mig_source(jax.random.fold_in(key_list[10], 71), 0)
    mig_pages = draw_mig_pages(jax.random.fold_in(key_list[10], 71), 0)
    return dict(new_queries=new_queries, new_keys=new_keys, new_values=new_values, key_pool=key_pool, value_pool=value_pool, lengths=lengths, page_table=page_table, mig_row=mig_row, mig_source=mig_source, mig_pages=mig_pages)


def attend(queries, fresh_keys, fresh_values, cache_keys, cache_values, row_lengths):
    row_count = queries.shape[0]
    groups = fresh_keys.shape[-1] // HD
    group_size = queries.shape[-1] // fresh_keys.shape[-1]
    query_f = queries.astype(jnp.float32).reshape(row_count, 2, groups, group_size, HD)
    keys_c = cache_keys.astype(jnp.float32).reshape(row_count, -1, groups, HD)
    values_c = cache_values.astype(jnp.float32).reshape(row_count, -1, groups, HD)
    keys_n = fresh_keys.astype(jnp.float32).reshape(row_count, 2, groups, HD)
    values_n = fresh_values.astype(jnp.float32).reshape(row_count, 2, groups, HD)
    score_scale = 1.0 / math.sqrt(HD)
    cache_scores = jnp.einsum('rskgd,rtkd->rskgt', query_f, keys_c) * score_scale
    positions = jnp.arange(keys_c.shape[1], dtype=jnp.int32)
    visible = positions[None, :] < row_lengths[:, None]
    cache_scores = jnp.where(visible[:, None, None, None, :], cache_scores, -jnp.inf)
    fresh_scores = jnp.einsum('rskgd,rjkd->rskgj', query_f, keys_n) * score_scale
    steps_idx = jnp.arange(2, dtype=jnp.int32)
    causal = steps_idx[None, :] <= steps_idx[:, None]
    fresh_scores = jnp.where(causal[None, :, None, None, :], fresh_scores, -jnp.inf)
    row_max = jnp.maximum(lax.optimization_barrier(jnp.max(cache_scores, axis=-1)), lax.optimization_barrier(jnp.max(fresh_scores, axis=-1)))[..., None]
    cache_exp = jnp.exp(cache_scores - row_max)
    fresh_exp = jnp.exp(fresh_scores - row_max)
    weight_sum = lax.optimization_barrier(jnp.sum(cache_exp, axis=-1, keepdims=True)) + lax.optimization_barrier(jnp.sum(fresh_exp, axis=-1, keepdims=True))
    cache_weights = (cache_exp / weight_sum).astype(jnp.bfloat16)
    fresh_weights = (fresh_exp / weight_sum).astype(jnp.bfloat16)
    mixed = jnp.einsum('rskgt,rtkd->rskgd', cache_weights.astype(jnp.float32), values_c)
    mixed = mixed + jnp.einsum('rskgj,rjkd->rskgd', fresh_weights.astype(jnp.float32), values_n)
    return mixed.astype(jnp.bfloat16).reshape(row_count, 2, -1)

def reference(new_queries, new_keys, new_values, key_pool, value_pool, lengths, page_table, mig_row, mig_source, mig_pages):
    target = (mig_row // ROWS).astype(jnp.int32)
    destination = (target[:, None] * POOL + page_table[mig_row]).reshape(-1).astype(jnp.int32)
    anchor = (mig_source[:, None] * POOL + mig_pages).reshape(-1).astype(jnp.int32)
    key_moved = key_pool.at[destination].set(key_pool[anchor])
    value_moved = value_pool.at[destination].set(value_pool[anchor])

    def one_instance(instance):
        first_row = (instance * ROWS).astype(jnp.int32)
        first_page = (instance * POOL).astype(jnp.int32)
        queries = lax.dynamic_slice_in_dim(new_queries, first_row, ROWS, 0)
        fresh_keys = lax.dynamic_slice_in_dim(new_keys, first_row, ROWS, 0)
        fresh_values = lax.dynamic_slice_in_dim(new_values, first_row, ROWS, 0)
        table = lax.dynamic_slice_in_dim(page_table, first_row, ROWS, 0)
        row_lengths = lax.dynamic_slice_in_dim(lengths, first_row, ROWS, 0)
        pool_keys = lax.dynamic_slice_in_dim(key_moved, first_page, POOL, 0)
        pool_values = lax.dynamic_slice_in_dim(value_moved, first_page, POOL, 0)
        return attend(queries, fresh_keys, fresh_values, pool_keys[table], pool_values[table], row_lengths)
    outputs = lax.map(one_instance, jnp.arange(N_INST, dtype=jnp.int32))
    attention = outputs.reshape(N_INST * ROWS, 2, HQ * HD)
    return (attention, key_moved, value_moved)
```

```python
import functools
import math

import jax
import jax.numpy as jnp
from jax import lax
from jax.experimental import pallas as pl
from jax.experimental.pallas import tpu as pltpu
from jax.sharding import Mesh
from jax.sharding import PartitionSpec as P

HD = 128
PAGE = 128
MAXP = 4
ROWS = 16
POOL = 64
MOVES = 11
MIGS = 352
NX = 4
NZ = 2
TP = 8
GROUP = 8
SPREAD = 16
PIECES = SPREAD * MOVES
WIDTH = 256
CAPS = (96, 112, 144, PIECES)
HALVES = 1
PR = PAGE * MAXP // SPREAD // HALVES
QKV = 48
VMEM = pltpu.VMEM
SMEM = pltpu.SMEM
LIMIT = pltpu.CompilerParams(vmem_limit_bytes=40 * 1024 * 1024)


def spec(space):
    return pl.BlockSpec(memory_space=space)


def cost(bytes_accessed, flops=0):
    return pl.CostEstimate(flops=flops, bytes_accessed=bytes_accessed, transcendentals=0)


def place_of(inst):
    half = (inst >> 2) & 1
    place = ((inst >> 3) << 2) | (inst & 3)
    return half, place


def plan_kernel(own_ref, row_ref, src_ref, pages_ref, table_ref, out_ref):
    own = own_ref[0]
    half, _ = place_of(own)
    sub = lax.broadcasted_iota(jnp.int32, (MIGS, MIGS), 0)
    lane = lax.broadcasted_iota(jnp.int32, (MIGS, MIGS), 1)

    def to_column(row):
        spread = jnp.where(sub == lane, row.astype(jnp.float32), 0.0)
        return jnp.sum(spread, axis=1, keepdims=True).astype(jnp.int32)

    def rank(same):
        counted = jnp.where((lane < sub) & same, 1.0, 0.0)
        return jnp.sum(counted, axis=1, keepdims=True).astype(jnp.int32)

    row_r, src_r = row_ref[...], src_ref[...]
    row_c, src_c = to_column(row_r), to_column(src_r)
    tgt_r, tgt_c = row_r >> 4, row_c >> 4
    sh_r, _ = place_of(src_r)
    th_r, _ = place_of(tgt_r)
    sh_c, sp_c = place_of(src_c)
    th_c, tp_c = place_of(tgt_c)
    rank_src = rank(src_c == src_r)
    rank_tgt = rank(tgt_c == tgt_r)
    rank_cross = rank((sh_c == sh_r) & (sh_r != th_r))
    src_place = sp_c * MOVES + rank_src
    final_place = tp_c * MOVES + rank_tgt
    col = lax.broadcasted_iota(jnp.int32, (1, WIDTH), 1)
    message, page = col >> 2, col & 3

    def pick(chosen, value):
        picked = jnp.where(chosen, value.astype(jnp.float32), 0.0)
        return jnp.sum(picked, axis=0, keepdims=True).astype(jnp.int32)

    leaves = (sh_c == half) & (th_c != half)
    out_ref[0:1, :] = pick(leaves & (rank_cross == col), src_place)
    origin = jnp.where(sh_c == half, src_place, PIECES + rank_cross)
    out_ref[1:2, :] = pick((th_c == half) & (final_place == col), origin)
    pages = pages_ref[...]
    by_page = pages[:, 3:4]
    for j in range(MAXP - 1):
        by_page = jnp.where(page == j, pages[:, j : j + 1], by_page)
    out_ref[2:3, :] = pick((src_c == own) & (rank_src == message), by_page)
    arrival = pick((tgt_c == own) & (rank_tgt == message), row_c & (ROWS - 1))
    table = table_ref[...]
    by_page = table[:, 3:4]
    for j in range(MAXP - 1):
        by_page = jnp.where(page == j, table[:, j : j + 1], by_page)
    row_id = lax.broadcasted_iota(jnp.int32, (ROWS, WIDTH), 0)
    out_ref[3:4, :] = pick(row_id == arrival, by_page)
    out_ref[4:5, :] = arrival
    out_ref[5:6, :] = pick(leaves & (col >= 0), jnp.ones_like(src_place))
    out_ref[6:8, :] = jnp.zeros((2, WIDTH), jnp.int32)


def make_plan(own, mig_row, mig_source, mig_pages, page_table):
    return pl.pallas_call(
        plan_kernel,
        out_shape=jax.ShapeDtypeStruct((8, WIDTH), jnp.int32),
        in_specs=[spec(SMEM), spec(VMEM), spec(VMEM), spec(VMEM), spec(VMEM)],
        out_specs=spec(VMEM),
        compiler_params=LIMIT,
        cost_estimate=cost(100_000),
    )(own, mig_row.reshape(1, MIGS), mig_source.reshape(1, MIGS), mig_pages, page_table)


def pack_kernel(q_ref, k_ref, v_ref, out_ref, scratch):
    scratch[...] = jnp.zeros_like(scratch)
    for d in range(TP):
        for r in range(2):
            for g in range(GROUP):
                head = d * GROUP + g
                piece = q_ref[r, :, head * HD : (head + 1) * HD]
                scratch[d, r, 2 * g : 2 * g + 2, :] = piece.astype(jnp.float32)
            scratch[d, r, 16:18, :] = k_ref[r, :, d * HD : (d + 1) * HD].astype(jnp.float32)
            scratch[d, r, 32:34, :] = v_ref[r, :, d * HD : (d + 1) * HD].astype(jnp.float32)
    out_ref[...] = scratch[...].astype(jnp.bfloat16)


def pack(new_queries, new_keys, new_values):
    return pl.pallas_call(
        pack_kernel,
        out_shape=jax.ShapeDtypeStruct((TP, 2, QKV, HD), jnp.bfloat16),
        in_specs=[spec(VMEM)] * 3,
        out_specs=spec(VMEM),
        scratch_shapes=[pltpu.VMEM((TP, 2, QKV, HD), jnp.float32)],
        compiler_params=LIMIT,
        cost_estimate=cost(400_000),
    )(new_queries, new_keys, new_values)


def unpack_kernel(in_ref, out_ref):
    for d in range(TP):
        for r in range(2):
            block = in_ref[d, r].astype(jnp.float32)
            for g in range(GROUP):
                head = d * GROUP + g
                piece = block[2 * g : 2 * g + 2, :]
                out_ref[r, :, head * HD : (head + 1) * HD] = piece.astype(jnp.bfloat16)


def unpack(received):
    return pl.pallas_call(
        unpack_kernel,
        out_shape=jax.ShapeDtypeStruct((2, 2, TP * GROUP * HD), jnp.bfloat16),
        in_specs=[spec(VMEM)],
        out_specs=spec(VMEM),
        compiler_params=LIMIT,
        cost_estimate=cost(200_000),
    )(received)


def send_kernel(part, plan_ref, pool_ref, out_ref, sem):
    copies = []
    for m in range(MOVES):
        for j in range(MAXP):
            copies.append(
                pltpu.make_async_copy(
                    pool_ref.at[plan_ref[2, m * MAXP + j], :, part],
                    out_ref.at[MAXP * j : MAXP * (j + 1), m],
                    sem.at[m * MAXP + j],
                )
            )
    for copy in copies:
        copy.start()
    for copy in copies:
        copy.wait()


def outgoing(plan, pool, part):
    return pl.pallas_call(
        functools.partial(send_kernel, part),
        out_shape=jax.ShapeDtypeStruct((SPREAD, MOVES, PR, HD), jnp.bfloat16),
        in_specs=[spec(SMEM), spec(pl.ANY)],
        out_specs=spec(VMEM),
        scratch_shapes=[pltpu.SemaphoreType.DMA((MOVES * MAXP,))],
        compiler_params=LIMIT,
        cost_estimate=cost(4_000_000 // HALVES),
    )(plan, pool.reshape(POOL, MAXP, HALVES, PR, HD))


def cross_kernel(cap, plan_ref, held_ref, out_ref):
    @pl.loop(0, cap, step=8)
    def _(base):
        for i in range(8):
            out_ref[base + i] = held_ref[plan_ref[0, base + i]]


def crossing(plan, held, cap):
    return pl.pallas_call(
        functools.partial(cross_kernel, cap),
        out_shape=jax.ShapeDtypeStruct((cap, PR, HD), jnp.bfloat16),
        in_specs=[spec(SMEM), spec(VMEM)],
        out_specs=spec(VMEM),
        compiler_params=LIMIT,
        cost_estimate=cost(4_000_000 // HALVES),
    )(plan, held)


def deliver_kernel(cap, plan_ref, held_ref, crossed_ref, out_ref):
    @pl.loop(0, PIECES, step=8)
    def _(base):
        for i in range(8):
            origin = plan_ref[1, base + i]
            kept = held_ref[jnp.minimum(origin, PIECES - 1)]
            crossed = crossed_ref[jnp.clip(origin - PIECES, 0, cap - 1)]
            out_ref[base + i] = jnp.where(origin < PIECES, kept, crossed)


def deliver(plan, held, crossed, cap):
    return pl.pallas_call(
        functools.partial(deliver_kernel, cap),
        out_shape=jax.ShapeDtypeStruct((PIECES, PR, HD), jnp.bfloat16),
        in_specs=[spec(SMEM), spec(VMEM), spec(VMEM)],
        out_specs=spec(VMEM),
        compiler_params=LIMIT,
        cost_estimate=cost(6_000_000 // HALVES),
    )(plan, held, crossed)


def place_pages(plan_ref, pool_ref, received_refs, out_ref):
    out_ref[...] = pool_ref[...]

    @pl.loop(0, MOVES)
    def _(k):
        for j in range(MAXP):
            page = plan_ref[3, k * MAXP + j]
            for quarter in range(MAXP):
                for part, received_ref in enumerate(received_refs):
                    first = (quarter * HALVES + part) * PR
                    out_ref[page, first : first + PR, :] = received_ref[MAXP * j + quarter, k]


def keys_kernel(own_ref, plan_ref, table_ref, lengths_ref, qkv_ref, pool_ref, *refs):
    received_refs, (moved_ref, cache_ref, fresh_ref) = refs[:HALVES], refs[HALVES:]
    place_pages(plan_ref, pool_ref, received_refs, moved_ref)
    scale = 1.0 / math.sqrt(HD)
    position = lax.broadcasted_iota(jnp.int32, (16, MAXP * PAGE), 1)
    fresh_index = lax.broadcasted_iota(jnp.int32, (16, 16), 1)
    step = lax.broadcasted_iota(jnp.int32, (16, 16), 0) & 1
    by_rows = (((1,), (1,)), ((), ()))

    @pl.loop(0, ROWS, step=4)
    def _(base):
        for i in range(4):
            r = base + i
            queries = qkv_ref[r, 0:16, :]
            scores = jnp.concatenate(
                [
                    lax.dot_general(
                        queries,
                        moved_ref[table_ref[r, j]],
                        by_rows,
                        preferred_element_type=jnp.float32,
                    )
                    for j in range(MAXP)
                ],
                axis=1,
            )
            length = lengths_ref[own_ref[0] * ROWS + r]
            scores = jnp.where(position < length, scores * scale, -jnp.inf)
            fresh = lax.dot_general(
                queries, qkv_ref[r, 16:32, :], by_rows, preferred_element_type=jnp.float32
            )
            fresh = jnp.where(fresh_index <= step, fresh * scale, -jnp.inf)
            top = jnp.maximum(
                jnp.max(scores, axis=1, keepdims=True), jnp.max(fresh, axis=1, keepdims=True)
            )
            scores = jnp.exp(scores - top)
            fresh = jnp.exp(fresh - top)
            total = jnp.sum(scores, axis=1, keepdims=True) + jnp.sum(fresh, axis=1, keepdims=True)
            cache_ref[r] = (scores / total).astype(jnp.bfloat16)
            fresh_ref[r] = (fresh / total).astype(jnp.bfloat16)


def keys_step(own, plan, table, lengths, qkv, pool, received):
    return pl.pallas_call(
        keys_kernel,
        out_shape=(
            jax.ShapeDtypeStruct((POOL, PAGE, HD), jnp.bfloat16),
            jax.ShapeDtypeStruct((ROWS, 16, MAXP * PAGE), jnp.bfloat16),
            jax.ShapeDtypeStruct((ROWS, 16, 16), jnp.bfloat16),
        ),
        in_specs=[spec(SMEM)] * 4 + [spec(VMEM)] * (2 + HALVES),
        out_specs=(spec(VMEM),) * 3,
        compiler_params=LIMIT,
        cost_estimate=cost(16_000_000),
    )(own, plan, table, lengths, qkv, pool, *received)


def values_kernel(plan_ref, table_ref, cache_ref, fresh_ref, qkv_ref, pool_ref, *refs):
    received_refs, (moved_ref, out_ref) = refs[:HALVES], refs[HALVES:]
    place_pages(plan_ref, pool_ref, received_refs, moved_ref)
    for r in range(ROWS):
        mixed = jnp.dot(fresh_ref[r], qkv_ref[r, 32:48, :], preferred_element_type=jnp.float32)
        for j in range(MAXP):
            mixed += jnp.dot(
                cache_ref[r, :, j * PAGE : (j + 1) * PAGE],
                moved_ref[table_ref[r, j]],
                preferred_element_type=jnp.float32,
            )
        out_ref[r // 2, r % 2] = mixed.astype(jnp.bfloat16)


def values_step(plan, table, weights, fresh, qkv, pool, received):
    return pl.pallas_call(
        values_kernel,
        out_shape=(
            jax.ShapeDtypeStruct((POOL, PAGE, HD), jnp.bfloat16),
            jax.ShapeDtypeStruct((TP, 2, 16, HD), jnp.bfloat16),
        ),
        in_specs=[spec(SMEM)] * 2 + [spec(VMEM)] * (4 + HALVES),
        out_specs=(spec(VMEM),) * 2,
        compiler_params=LIMIT,
        cost_estimate=cost(12_000_000),
    )(plan, table, weights, fresh, qkv, pool, *received)


def swap(array, axes):
    return lax.all_to_all(array, axes, split_axis=0, concat_axis=0, tiled=True)


def move_and_attend(cap, own, plan, table, lengths, qkv, key_pool, value_pool):
    chunks = [(pool, part) for pool in (key_pool, value_pool) for part in range(HALVES)]
    held, crossed, received = [], [], []
    for pool, part in chunks:
        send = outgoing(plan, pool, part)
        if held:
            send, held[-1] = lax.optimization_barrier((send, held[-1]))
        held.append(swap(send, ("y", "x")).reshape(PIECES, PR, HD))
    for piece in held:
        leaving = crossing(plan, piece, cap)
        crossed.append(lax.ppermute(leaving, "zh", [(0, 1), (1, 0)]))
    for piece, other in zip(held, crossed):
        final = deliver(plan, piece, other, cap).reshape(SPREAD, MOVES, PR, HD)
        received.append(swap(final, ("y", "x")))
    key_moved, weights, fresh = keys_step(
        own, plan, table, lengths, qkv, key_pool, received[:HALVES]
    )
    value_moved, mixed = values_step(
        plan, table, weights, fresh, qkv, value_pool, received[HALVES:]
    )
    return mixed, key_moved, value_moved


def body(
    new_queries,
    new_keys,
    new_values,
    key_pool,
    value_pool,
    lengths,
    page_table,
    mig_row,
    mig_source,
    mig_pages,
):
    own = lax.axis_index(("y", "zh", "x")).astype(jnp.int32).reshape(1)
    plan = make_plan(own, mig_row, mig_source, mig_pages, page_table)
    qkv = swap(pack(new_queries, new_keys, new_values), ("zl", "c")).reshape(ROWS, QKV, HD)
    count = plan[5, 0]
    branch = sum((count > cap).astype(jnp.int32) for cap in CAPS[:-1])
    mixed, key_moved, value_moved = lax.switch(
        branch,
        [functools.partial(move_and_attend, cap) for cap in CAPS],
        own,
        plan,
        page_table,
        lengths,
        qkv,
        key_pool,
        value_pool,
    )
    attention = unpack(swap(mixed, ("zl", "c")))
    return (attention, key_moved, value_moved)


def solution(mesh):
    fine = Mesh(mesh.devices.reshape(4, NZ, NX, 4, 2), ("y", "zh", "x", "zl", "c"))
    inst, tp = ("y", "zh", "x"), ("zl", "c")
    rows = P(inst + tp, None, None)
    pool = P(inst, None, tp)
    return jax.shard_map(
        body,
        mesh=fine,
        in_specs=(rows, rows, rows, pool, pool, P(), P(inst, None), P(), P(), P()),
        out_specs=(rows, pool, pool),
        check_vma=False,
    )
```

```python
import functools
import math

import jax
import jax.numpy as jnp
from jax import lax
from jax.experimental import pallas as pl
from jax.experimental.pallas import tpu as pltpu
from jax.sharding import Mesh
from jax.sharding import PartitionSpec as P

HD = 128
PAGE = 128
MAXP = 4
ROWS = 16
POOL = 64
MOVES = 11
MIGS = 352
NX = 4
NZ = 2
TP = 8
GROUP = 8
SPREAD = 16
PIECES = SPREAD * MOVES
WIDTH = 256
BRANCHES = ((0, PIECES), (2, 64), (3, 48))
PR = PAGE * MAXP // SPREAD
QKV = 48
VMEM = pltpu.VMEM
SMEM = pltpu.SMEM
HBM = pltpu.HBM
FILLER = 100_000_000_000
LIMIT = pltpu.CompilerParams(vmem_limit_bytes=40 * 1024 * 1024)
ALONE = pltpu.CompilerParams(vmem_limit_bytes=63_400_000)


def spec(space):
    return pl.BlockSpec(memory_space=space)


def cost(bytes_accessed):
    return pl.CostEstimate(flops=100 * bytes_accessed, bytes_accessed=bytes_accessed, transcendentals=0)


def place_of(inst):
    half = (inst >> 2) & 1
    place = ((inst >> 3) << 2) | (inst & 3)
    return half, place


def plan_kernel(own_ref, row_ref, src_ref, pages_ref, table_ref, out_ref, branch_ref):
    own = own_ref[0] >> 3
    half, _ = place_of(own)
    sub = lax.broadcasted_iota(jnp.int32, (MIGS, MIGS), 0)
    lane = lax.broadcasted_iota(jnp.int32, (MIGS, MIGS), 1)

    def to_column(row):
        spread = jnp.where(sub == lane, row.astype(jnp.float32), 0.0)
        return jnp.sum(spread, axis=1, keepdims=True).astype(jnp.int32)

    def to_row(column):
        spread = jnp.where(sub == lane, column.astype(jnp.float32), 0.0)
        return jnp.sum(spread, axis=0, keepdims=True).astype(jnp.int32)

    def count(same):
        return jnp.sum(jnp.where(same, 1.0, 0.0), axis=1, keepdims=True).astype(jnp.int32)

    row_r = row_ref[...].reshape(1, MIGS)
    src_r = src_ref[...].reshape(1, MIGS)
    row_c, src_c = to_column(row_r), to_column(src_r)
    tgt_r, tgt_c = row_r >> 4, row_c >> 4
    sh_r, _ = place_of(src_r)
    th_r, _ = place_of(tgt_r)
    sh_c, sp_c = place_of(src_c)
    th_c, tp_c = place_of(tgt_c)
    before = lane < sub
    same_src = src_c == src_r
    crosses = sh_r != th_r
    rank_src = count(before & same_src)
    rank_tgt = count(before & (tgt_c == tgt_r))
    rank_out = count(before & same_src & crosses)
    fewest = jnp.min(count(same_src & crosses), axis=0, keepdims=True)
    total = jnp.sum(jnp.where((sh_c == 0) & (th_c == 1), 1.0, 0.0), axis=0, keepdims=True)
    total = total.astype(jnp.int32)
    branch = jnp.zeros((1, 1), jnp.int32)
    whole = jnp.full((1, 1), BRANCHES[0][0], jnp.int32)
    for index, (whole_i, cap) in enumerate(BRANCHES):
        fits = (fewest >= whole_i) & (total - SPREAD * whole_i <= cap)
        branch = jnp.where(fits, index, branch)
        whole = jnp.where(fits, whole_i, whole)
    crosses_c = sh_c != th_c
    direct = crosses_c & (rank_out < whole)
    later = crosses_c & (rank_out >= whole)
    rank_rest = rank_src - jnp.minimum(rank_out, whole)
    later_r = to_row(jnp.where(later, 1, 0)) > 0
    rank_later = count(before & later_r & (sh_c == sh_r))
    rest_place = sp_c * (MOVES - whole) + rank_rest
    direct_place = SPREAD * (MOVES - whole) + sp_c * whole + rank_out
    origin = jnp.where(sh_c == th_c, rest_place, PIECES + rank_later)
    origin = jnp.where(direct, direct_place, origin)
    final_place = tp_c * MOVES + rank_tgt
    col = lax.broadcasted_iota(jnp.int32, (1, WIDTH), 1)
    message, page = col >> 2, col & 3

    def pick(chosen, value):
        picked = jnp.where(chosen, value.astype(jnp.float32), 0.0)
        return jnp.sum(picked, axis=0, keepdims=True).astype(jnp.int32)

    def by_page(pages):
        chosen = pages[MAXP - 1]
        for j in range(MAXP - 1):
            chosen = jnp.where(page == j, pages[j], chosen)
        return chosen

    out_ref[0:1, :] = pick(later & (sh_c == half) & (rank_later == col), rest_place)
    out_ref[1:2, :] = pick((th_c == half) & (final_place == col), origin)
    pages = by_page([to_column(pages_ref[j : j + 1, :]) for j in range(MAXP)])
    mine = src_c == own
    out_ref[2:3, :] = pick(mine & ~direct & (rank_rest == message), pages)
    arrival = pick((tgt_c == own) & (rank_tgt == message), row_c & (ROWS - 1))
    sub16 = lax.broadcasted_iota(jnp.int32, (ROWS, ROWS), 0)
    lane16 = lax.broadcasted_iota(jnp.int32, (ROWS, ROWS), 1)

    def table_column(j):
        spread = jnp.where(sub16 == lane16, table_ref[j : j + 1, :].astype(jnp.float32), 0.0)
        return jnp.sum(spread, axis=1, keepdims=True).astype(jnp.int32)

    table = by_page([table_column(j) for j in range(MAXP)])
    row_id = lax.broadcasted_iota(jnp.int32, (ROWS, WIDTH), 0)
    out_ref[3:4, :] = pick(row_id == arrival, table)
    out_ref[4:5, :] = pick(mine & direct & (rank_out == message), pages)
    out_ref[5:6, :] = jnp.zeros((1, WIDTH), jnp.int32)
    branch_ref[0] = branch[0, 0]
    out_ref[6:7, :] = pick((tgt_c == own) & ((row_c & (ROWS - 1)) == col), rank_tgt + 1) - 1
    out_ref[7:8, :] = jnp.zeros((1, WIDTH), jnp.int32)


def make_plan(own, mig_row, mig_source, mig_pages, page_table):
    return pl.pallas_call(
        plan_kernel,
        out_shape=(
            jax.ShapeDtypeStruct((8, WIDTH), jnp.int32),
            jax.ShapeDtypeStruct((1,), jnp.int32),
        ),
        in_specs=[spec(SMEM), spec(VMEM), spec(VMEM), spec(VMEM), spec(VMEM)],
        out_specs=(spec(VMEM), spec(SMEM)),
        compiler_params=ALONE,
        cost_estimate=cost(100_000),
    )(own, mig_row, mig_source, mig_pages.T, page_table.T)


def pack_kernel(own_ref, q_ref, k_ref, v_ref, after_ref, *refs):
    blocks, scratch = refs[:TP], refs[TP]
    scratch[...] = jnp.zeros_like(scratch)
    place = own_ref[0] & (TP - 1)

    @pl.loop(0, TP)
    def _(k):
        d = place ^ k
        own_head = pl.ds(pl.multiple_of(d * HD, HD), HD)
        for r in range(2):
            for g in range(GROUP):
                head = pl.ds(pl.multiple_of((d * GROUP + g) * HD, HD), HD)
                scratch[k, r, 2 * g : 2 * g + 2, :] = q_ref[r, :, head].astype(jnp.float32)
            scratch[k, r, 16:18, :] = k_ref[r, :, own_head].astype(jnp.float32)
            scratch[k, r, 32:34, :] = v_ref[r, :, own_head].astype(jnp.float32)

    for k in range(TP):
        blocks[k][...] = scratch[k].astype(jnp.bfloat16)


def pack(own, new_queries, new_keys, new_values, after):
    return pl.pallas_call(
        pack_kernel,
        out_shape=(jax.ShapeDtypeStruct((2, QKV, HD), jnp.bfloat16),) * TP,
        in_specs=[spec(SMEM)] + [spec(VMEM)] * 3 + [spec(pl.ANY)],
        out_specs=(spec(VMEM),) * TP,
        scratch_shapes=[pltpu.VMEM((TP, 2, QKV, HD), jnp.float32)],
        compiler_params=LIMIT,
        cost_estimate=cost(400_000),
    )(own, new_queries, new_keys, new_values, after)


def unpack_kernel(in_ref, out_ref):
    for d in range(TP):
        for r in range(2):
            block = in_ref[d, r].astype(jnp.float32)
            for g in range(GROUP):
                head = d * GROUP + g
                piece = block[2 * g : 2 * g + 2, :]
                out_ref[r, :, head * HD : (head + 1) * HD] = piece.astype(jnp.bfloat16)


def unpack(received):
    return pl.pallas_call(
        unpack_kernel,
        out_shape=jax.ShapeDtypeStruct((2, 2, TP * GROUP * HD), jnp.bfloat16),
        in_specs=[spec(VMEM)],
        out_specs=spec(VMEM),
        compiler_params=ALONE,
        cost_estimate=cost(200_000),
    )(received)


def send_kernel(whole, plan_ref, keys_ref, values_ref, *refs):
    rest = MOVES - whole
    if whole:
        direct_ref, *refs = refs
    out_ref, held, in_sem, out_sem = refs
    pools = (keys_ref, values_ref)
    loads = []

    def load(row, m, j, target):
        for part, pool in enumerate(pools):
            source = pool.at[plan_ref[row, m * MAXP + j]]
            slot = target.at[pl.ds(MAXP * j, MAXP), m, part]
            copy = pltpu.make_async_copy(source, slot, in_sem.at[len(loads)])
            copy.start()
            loads.append(copy)

    for j in range(MAXP):
        for m in range(rest):
            load(2, m, j, held)
    for j in range(MAXP):
        for m in range(whole):
            load(4, m, j, direct_ref)
    sends = []
    for j in range(MAXP):
        for copy in loads[2 * rest * j : 2 * rest * (j + 1)]:
            copy.wait()
        block = pl.ds(MAXP * j, MAXP)
        send = pltpu.make_async_copy(held.at[block], out_ref.at[block], out_sem.at[j])
        send.start()
        sends.append(send)
    for copy in loads[2 * rest * MAXP :] + sends:
        copy.wait()


def outgoing(plan, keys, values, whole):
    rest = MOVES - whole
    held = (SPREAD, rest, 2, PR, HD)
    shapes = [(SPREAD, whole, 2, PR, HD), held] if whole else [held]
    pools = [p.reshape(POOL, MAXP, PR, HD) for p in (keys, values)]
    outs = pl.pallas_call(
        functools.partial(send_kernel, whole),
        out_shape=tuple(jax.ShapeDtypeStruct(shape, jnp.bfloat16) for shape in shapes),
        in_specs=[spec(SMEM)] + [spec(pl.ANY)] * 2,
        out_specs=((spec(VMEM),) if whole else ()) + (spec(HBM),),
        scratch_shapes=[
            pltpu.VMEM(held, jnp.bfloat16),
            pltpu.SemaphoreType.DMA((2 * MAXP * MOVES,)),
            pltpu.SemaphoreType.DMA((MAXP,)),
        ],
        compiler_params=ALONE,
        cost_estimate=cost(6_000_000),
    )(plan, *pools)
    return outs if whole else (None, outs[0])


def touch_kernel(array_ref, out_ref):
    out_ref[...] = jnp.zeros_like(out_ref)


def touch(array):
    return pl.pallas_call(
        touch_kernel,
        out_shape=jax.ShapeDtypeStruct((8, HD), jnp.float32),
        in_specs=[spec(pl.ANY)],
        out_specs=spec(VMEM),
        compiler_params=ALONE,
        cost_estimate=cost(FILLER),
    )(array)


def cross_kernel(cap, plan_ref, held_ref, *refs):
    keys_ref, values_ref = refs[-2:]

    @pl.loop(0, cap, step=4)
    def _(base):
        for i in range(4):
            place = plan_ref[0, base + i]
            keys_ref[base + i] = held_ref[place, 0]
            values_ref[base + i] = held_ref[place, 1]


def crossing(plan, held, cap, *through):
    piece = jax.ShapeDtypeStruct((cap, PR, HD), jnp.bfloat16)
    kept = [jax.ShapeDtypeStruct(a.shape, a.dtype) for a in through[:1]]
    outs = pl.pallas_call(
        functools.partial(cross_kernel, cap),
        out_shape=tuple(kept + [piece, piece]),
        in_specs=[spec(SMEM), spec(VMEM)] + [spec(pl.ANY)] * len(through),
        out_specs=(spec(pl.ANY),) * len(kept) + (spec(VMEM),) * 2,
        input_output_aliases={2: 0} if kept else {},
        compiler_params=ALONE,
        cost_estimate=cost(4_000_000),
    )(plan, held, *through)
    return outs if kept else (None, *outs)


def deliver_kernel(whole, part, unread, plan_ref, *refs):
    refs, (out_ref, gathered, ordered, in_sem, out_sem) = refs[: -5 - unread], refs[-5:]
    kept = SPREAD * (MOVES - whole)
    if whole:
        rest_ref, direct_ref, later_ref = refs
        moves = [
            (rest_ref.at[:, part], gathered.at[0:kept]),
            (direct_ref.at[:, part], gathered.at[kept:PIECES]),
            (later_ref, gathered.at[PIECES:]),
        ]
    else:
        rest_ref, later_ref = refs
        moves = [(rest_ref.at[:, part], gathered.at[0:kept]), (later_ref, gathered.at[PIECES:])]
    copies = [pltpu.make_async_copy(a, b, in_sem.at[i]) for i, (a, b) in enumerate(moves)]
    for copy in copies:
        copy.start()
    for copy in copies:
        copy.wait()
    step = PIECES // 4
    sends = []
    for quarter in range(4):
        first = quarter * step

        @pl.loop(first, first + step, step=4)
        def _(base):
            for i in range(4):
                ordered[base + i] = gathered[plan_ref[1, base + i]]

        block = pl.ds(first, step)
        send = pltpu.make_async_copy(ordered.at[block], out_ref.at[block], out_sem.at[quarter])
        send.start()
        sends.append(send)
    for send in sends:
        send.wait()


def deliver(plan, rest, direct, later, cap, whole, part, beside, *after):
    arrays = [rest, direct, later] if whole else [rest, later]
    return pl.pallas_call(
        functools.partial(deliver_kernel, whole, part, len(after)),
        out_shape=jax.ShapeDtypeStruct((PIECES, PR, HD), jnp.bfloat16),
        in_specs=[spec(SMEM)] + [spec(pl.ANY)] * (len(arrays) + len(after)),
        out_specs=spec(HBM),
        scratch_shapes=[
            pltpu.VMEM((PIECES + cap, PR, HD), jnp.bfloat16),
            pltpu.VMEM((PIECES, PR, HD), jnp.bfloat16),
            pltpu.SemaphoreType.DMA((3,)),
            pltpu.SemaphoreType.DMA((4,)),
        ],
        compiler_params=ALONE,
        cost_estimate=cost(beside),
    )(plan, *arrays, *after)


def place_pages(plan_ref, pool_ref, received_ref, out_ref):
    out_ref[...] = pool_ref[...]

    @pl.loop(0, MOVES)
    def _(k):
        for j in range(MAXP):
            page = plan_ref[3, k * MAXP + j]
            for quarter in range(MAXP):
                first = quarter * PR
                out_ref[page, first : first + PR, :] = received_ref[MAXP * j + quarter, k]


def keys_kernel(own_ref, plan_ref, table_ref, lengths_ref, pool_ref, received_ref, *refs):
    blocks, (moved_ref, cache_ref, fresh_ref, qkv) = refs[:TP], refs[TP:]
    place_pages(plan_ref, pool_ref, received_ref, moved_ref)
    scale = 1.0 / math.sqrt(HD)
    position = lax.broadcasted_iota(jnp.int32, (16, MAXP * PAGE), 1)
    fresh_index = lax.broadcasted_iota(jnp.int32, (16, 16), 1)
    step = lax.broadcasted_iota(jnp.int32, (16, 16), 0) & 1
    by_rows = (((1,), (1,)), ((), ()))
    first_row = (own_ref[0] >> 3) * ROWS
    place = own_ref[0] & (TP - 1)
    for k in range(TP):
        qkv[pl.ds((place ^ k) * 2, 2)] = blocks[k][...]

    def attend(r):
        queries = qkv[r, 0:16, :]
        scores = jnp.concatenate(
            [
                lax.dot_general(
                    queries,
                    moved_ref[table_ref[j, r]],
                    by_rows,
                    preferred_element_type=jnp.float32,
                )
                for j in range(MAXP)
            ],
            axis=1,
        )
        scores = jnp.where(position < lengths_ref[first_row + r], scores * scale, -jnp.inf)
        fresh = lax.dot_general(
            queries, qkv[r, 16:32, :], by_rows, preferred_element_type=jnp.float32
        )
        fresh = jnp.where(fresh_index <= step, fresh * scale, -jnp.inf)
        top = jnp.maximum(
            jnp.max(scores, axis=1, keepdims=True), jnp.max(fresh, axis=1, keepdims=True)
        )
        scores = jnp.exp(scores - top)
        fresh = jnp.exp(fresh - top)
        total = jnp.sum(scores, axis=1, keepdims=True) + jnp.sum(fresh, axis=1, keepdims=True)
        cache_ref[r] = (scores / total).astype(jnp.bfloat16)
        fresh = (fresh / total).astype(jnp.bfloat16).astype(jnp.float32)
        values = qkv[r, 32:48, :].astype(jnp.float32)
        fresh_ref[r] = fresh[:, 0:1] * values[0:1, :] + fresh[:, 1:2] * values[1:2, :]

    @pl.loop(0, ROWS, step=4)
    def _(base):
        for i in range(4):
            attend(base + i)


def keys_step(own, plan, table, lengths, pool, received, blocks):
    return pl.pallas_call(
        keys_kernel,
        out_shape=(
            jax.ShapeDtypeStruct((POOL, PAGE, HD), jnp.bfloat16),
            jax.ShapeDtypeStruct((ROWS, 16, MAXP * PAGE), jnp.bfloat16),
            jax.ShapeDtypeStruct((ROWS, 16, HD), jnp.float32),
        ),
        in_specs=[spec(SMEM)] * 4 + [spec(VMEM)] * (2 + TP),
        out_specs=(spec(VMEM),) * 3,
        scratch_shapes=[pltpu.VMEM((ROWS, QKV, HD), jnp.bfloat16)],
        compiler_params=LIMIT,
        cost_estimate=cost(FILLER),
    )(own, plan, table, lengths, pool, received, *blocks)


def values_kernel(plan_ref, table_ref, cache_ref, fresh_ref, pool_ref, received_ref, out_ref):
    for r in range(ROWS):
        arrival = plan_ref[6, r]
        mixed = fresh_ref[r]
        for j in range(MAXP):
            arrived = received_ref[MAXP * j : MAXP * (j + 1), jnp.maximum(arrival, 0)]
            values = jnp.where(arrival >= 0, arrived.reshape(PAGE, HD), pool_ref[table_ref[j, r]])
            mixed += jnp.dot(
                cache_ref[r, :, j * PAGE : (j + 1) * PAGE],
                values,
                preferred_element_type=jnp.float32,
            )
        out_ref[r // 2, r % 2] = mixed.astype(jnp.bfloat16)


def values_step(plan, table, weights, fresh, pool, received):
    return pl.pallas_call(
        values_kernel,
        out_shape=jax.ShapeDtypeStruct((TP, 2, 16, HD), jnp.bfloat16),
        in_specs=[spec(SMEM)] * 2 + [spec(VMEM)] * 4,
        out_specs=spec(VMEM),
        compiler_params=LIMIT,
        cost_estimate=cost(4_000_000),
    )(plan, table, weights, fresh, pool, received)


def place_step(plan, pool, received):
    return pl.pallas_call(
        place_pages,
        out_shape=jax.ShapeDtypeStruct((POOL, PAGE, HD), jnp.bfloat16),
        in_specs=[spec(SMEM)] + [spec(VMEM)] * 2,
        out_specs=spec(VMEM),
        compiler_params=LIMIT,
        cost_estimate=cost(8_000_000),
    )(plan, pool, received)


def swap(array, axes):
    return lax.all_to_all(array, axes, split_axis=0, concat_axis=0, tiled=True)


def cross(array):
    return lax.ppermute(array, "zh", [(0, 1), (1, 0)])


def move_and_attend(
    whole, cap, own, plan, table, lengths, new_queries, new_keys, new_values, key_pool, value_pool
):
    kept = SPREAD * (MOVES - whole)
    direct, send = outgoing(plan, key_pool, value_pool, whole)
    crossed = []
    if whole:
        direct = cross(direct)
        crossed = [direct, touch(direct)]
    held = swap(send, ("y", "x")).reshape(kept, 2, PR, HD)
    through, leaving_keys, leaving_values = crossing(plan, held, cap, *crossed)
    later_keys, later_values = cross(leaving_keys), cross(leaving_values)
    if whole:
        direct = swap(through, ("y", "x")).reshape(SPREAD * whole, 2, PR, HD)
    final_keys = deliver(
        plan, held, direct, later_keys, cap, whole, 0, 4_000_000, touch(later_keys)
    )
    received_keys = swap(final_keys.reshape(SPREAD, MOVES, PR, HD), ("y", "x"))
    final_values = deliver(plan, held, direct, later_values, cap, whole, 1, FILLER)
    blocks = list(pack(own, new_queries, new_keys, new_values, final_values))
    for k in range(1, TP):
        blocks[k] = lax.ppermute(blocks[k], ("zl", "c"), [(i, i ^ k) for i in range(TP)])
    received_values = swap(final_values.reshape(SPREAD, MOVES, PR, HD), ("y", "x"))
    key_moved, weights, fresh = keys_step(
        own, plan, table, lengths, key_pool, received_keys, blocks
    )
    return key_moved, weights, fresh, received_values


def body(
    new_queries,
    new_keys,
    new_values,
    key_pool,
    value_pool,
    lengths,
    page_table,
    mig_row,
    mig_source,
    mig_pages,
):
    own = lax.axis_index(("y", "zh", "x", "zl", "c")).astype(jnp.int32).reshape(1)
    plan, branch = make_plan(own, mig_row, mig_source, mig_pages, page_table)
    table = page_table.T
    key_moved, weights, fresh, received_values = lax.switch(
        branch[0],
        [functools.partial(move_and_attend, whole, cap) for whole, cap in BRANCHES],
        own,
        plan,
        table,
        lengths,
        new_queries,
        new_keys,
        new_values,
        key_pool,
        value_pool,
    )
    mixed = values_step(plan, table, weights, fresh, value_pool, received_values)
    attention = unpack(swap(mixed, ("zl", "c")))
    value_moved = place_step(plan, value_pool, received_values)
    return (attention, key_moved, value_moved)


def solution(mesh):
    fine = Mesh(mesh.devices.reshape(4, NZ, NX, 4, 2), ("y", "zh", "x", "zl", "c"))
    inst, tp = ("y", "zh", "x"), ("zl", "c")
    rows = P(inst + tp, None, None)
    pool = P(inst, None, tp)
    return jax.shard_map(
        body,
        mesh=fine,
        in_specs=(rows, rows, rows, pool, pool, P(), P(inst, None), P(), P(), P()),
        out_specs=(rows, pool, pool),
        check_vma=False,
    )
```

```python
import functools
import math

import jax
import jax.numpy as jnp
from jax import lax
from jax.experimental import pallas as pl
from jax.experimental.pallas import tpu as pltpu
from jax.sharding import Mesh
from jax.sharding import PartitionSpec as P

HD = 128
PAGE = 128
MAXP = 4
ROWS = 16
POOL = 64
MOVES = 11
MIGS = 352
NX = 4
NZ = 2
TP = 8
GROUP = 8
SPREAD = 16
PIECES = SPREAD * MOVES
WIDTH = 256
WHOLE = 3
BRANCHES = ((MOVES, SPREAD * (MOVES - WHOLE)), (MOVES - 2, 52), (MOVES - 3, 48))
PR = PAGE * MAXP // SPREAD
QKV = 48
VMEM = pltpu.VMEM
SMEM = pltpu.SMEM
HBM = pltpu.HBM
FILLER = 100_000_000_000
LIMIT = pltpu.CompilerParams(vmem_limit_bytes=40 * 1024 * 1024)
ALONE = pltpu.CompilerParams(vmem_limit_bytes=63_400_000)


def spec(space):
    return pl.BlockSpec(memory_space=space)


def cost(bytes_accessed):
    return pl.CostEstimate(flops=100 * bytes_accessed, bytes_accessed=bytes_accessed, transcendentals=0)


def place_of(inst):
    half = (inst >> 2) & 1
    place = ((inst >> 3) << 2) | (inst & 3)
    return half, place


def plan_kernel(own_ref, row_ref, src_ref, pages_ref, table_ref, out_ref, branch_ref):
    own = own_ref[0] >> 3
    half, _ = place_of(own)
    sub = lax.broadcasted_iota(jnp.int32, (MIGS, MIGS), 0)
    lane = lax.broadcasted_iota(jnp.int32, (MIGS, MIGS), 1)

    def to_column(row):
        spread = jnp.where(sub == lane, row.astype(jnp.float32), 0.0)
        return jnp.sum(spread, axis=1, keepdims=True).astype(jnp.int32)

    def to_row(column):
        spread = jnp.where(sub == lane, column.astype(jnp.float32), 0.0)
        return jnp.sum(spread, axis=0, keepdims=True).astype(jnp.int32)

    def count(same):
        return jnp.sum(jnp.where(same, 1.0, 0.0), axis=1, keepdims=True).astype(jnp.int32)

    row_r = row_ref[...].reshape(1, MIGS)
    src_r = src_ref[...].reshape(1, MIGS)
    row_c, src_c = to_column(row_r), to_column(src_r)
    tgt_r, tgt_c = row_r >> 4, row_c >> 4
    sh_r, _ = place_of(src_r)
    th_r, _ = place_of(tgt_r)
    sh_c, sp_c = place_of(src_c)
    th_c, tp_c = place_of(tgt_c)
    before = lane < sub
    same_src = src_c == src_r
    crosses = sh_r != th_r
    rank_src = count(before & same_src)
    rank_tgt = count(before & (tgt_c == tgt_r))
    rank_out = count(before & same_src & crosses)
    fewest = jnp.min(count(same_src & crosses), axis=0, keepdims=True)
    crosses_c = sh_c != th_c
    direct = crosses_c & (rank_out < WHOLE)
    later = crosses_c & (rank_out >= WHOLE)
    needed = jnp.zeros((1, 1), jnp.float32)
    for side in range(NZ):
        leaving = jnp.where(later & (sh_c == side), 1.0, 0.0)
        needed = jnp.maximum(needed, jnp.sum(leaving, axis=0, keepdims=True))
    needed = needed.astype(jnp.int32)
    branch = jnp.zeros((1, 1), jnp.int32)
    slots = jnp.full((1, 1), BRANCHES[0][0], jnp.int32)
    for index, (slots_i, cap) in enumerate(BRANCHES):
        fits = (jnp.minimum(fewest, WHOLE) >= MOVES - slots_i) & (needed <= cap)
        branch = jnp.where(fits, index, branch)
        slots = jnp.where(fits, slots_i, slots)
    rank_rest = rank_src - jnp.minimum(rank_out, WHOLE)
    later_r = to_row(jnp.where(later, 1, 0)) > 0
    rank_later = count(before & later_r & (sh_c == sh_r))
    rest_place = sp_c * slots + rank_rest
    direct_place = SPREAD * slots + sp_c * WHOLE + rank_out
    origin = jnp.where(sh_c == th_c, rest_place, SPREAD * (slots + WHOLE) + rank_later)
    origin = jnp.where(direct, direct_place, origin)
    final_place = tp_c * MOVES + rank_tgt
    col = lax.broadcasted_iota(jnp.int32, (1, WIDTH), 1)
    message, page = col >> 2, col & 3

    def pick(chosen, value):
        picked = jnp.where(chosen, value.astype(jnp.float32), 0.0)
        return jnp.sum(picked, axis=0, keepdims=True).astype(jnp.int32)

    def by_page(pages):
        chosen = pages[MAXP - 1]
        for j in range(MAXP - 1):
            chosen = jnp.where(page == j, pages[j], chosen)
        return chosen

    out_ref[0:1, :] = pick(later & (sh_c == half) & (rank_later == col), rest_place)
    out_ref[1:2, :] = pick((th_c == half) & (final_place == col), origin)
    pages = by_page([to_column(pages_ref[j : j + 1, :]) for j in range(MAXP)])
    mine = src_c == own
    out_ref[2:3, :] = pick(mine & ~direct & (rank_rest == message), pages)
    arrival = pick((tgt_c == own) & (rank_tgt == message), row_c & (ROWS - 1))
    sub16 = lax.broadcasted_iota(jnp.int32, (ROWS, ROWS), 0)
    lane16 = lax.broadcasted_iota(jnp.int32, (ROWS, ROWS), 1)

    def table_column(j):
        spread = jnp.where(sub16 == lane16, table_ref[j : j + 1, :].astype(jnp.float32), 0.0)
        return jnp.sum(spread, axis=1, keepdims=True).astype(jnp.int32)

    table = by_page([table_column(j) for j in range(MAXP)])
    row_id = lax.broadcasted_iota(jnp.int32, (ROWS, WIDTH), 0)
    out_ref[3:4, :] = pick(row_id == arrival, table)
    out_ref[4:5, :] = pick(mine & direct & (rank_out == message), pages)
    out_ref[5:6, :] = arrival
    branch_ref[0] = branch[0, 0]
    out_ref[6:7, :] = pick((tgt_c == own) & ((row_c & (ROWS - 1)) == col), rank_tgt + 1) - 1
    out_ref[7:8, :] = jnp.zeros((1, WIDTH), jnp.int32)


def make_plan(own, mig_row, mig_source, mig_pages, page_table):
    return pl.pallas_call(
        plan_kernel,
        out_shape=(
            jax.ShapeDtypeStruct((8, WIDTH), jnp.int32),
            jax.ShapeDtypeStruct((1,), jnp.int32),
        ),
        in_specs=[spec(SMEM), spec(VMEM), spec(VMEM), spec(VMEM), spec(VMEM)],
        out_specs=(spec(VMEM), spec(SMEM)),
        compiler_params=ALONE,
        cost_estimate=cost(100_000),
    )(own, mig_row, mig_source, mig_pages.T, page_table.T)


def pack_kernel(own_ref, q_ref, k_ref, v_ref, after_ref, *refs):
    blocks, scratch = refs[:TP], refs[TP]
    scratch[...] = jnp.zeros_like(scratch)
    place = own_ref[0] & (TP - 1)

    @pl.loop(0, TP)
    def _(k):
        d = place ^ k
        own_head = pl.ds(pl.multiple_of(d * HD, HD), HD)
        for r in range(2):
            for g in range(GROUP):
                head = pl.ds(pl.multiple_of((d * GROUP + g) * HD, HD), HD)
                scratch[k, r, 2 * g : 2 * g + 2, :] = q_ref[r, :, head].astype(jnp.float32)
            scratch[k, r, 16:18, :] = k_ref[r, :, own_head].astype(jnp.float32)
            scratch[k, r, 32:34, :] = v_ref[r, :, own_head].astype(jnp.float32)

    for k in range(TP):
        blocks[k][...] = scratch[k].astype(jnp.bfloat16)


def pack(own, new_queries, new_keys, new_values, after):
    return pl.pallas_call(
        pack_kernel,
        out_shape=(jax.ShapeDtypeStruct((2, QKV, HD), jnp.bfloat16),) * TP,
        in_specs=[spec(SMEM)] + [spec(VMEM)] * 3 + [spec(pl.ANY)],
        out_specs=(spec(VMEM),) * TP,
        scratch_shapes=[pltpu.VMEM((TP, 2, QKV, HD), jnp.float32)],
        compiler_params=LIMIT,
        cost_estimate=cost(400_000),
    )(own, new_queries, new_keys, new_values, after)


def load_pages(plan_ref, row, messages, pools, target, sem):
    loads = []
    for j in range(MAXP):
        for m in range(messages):
            for part, pool in enumerate(pools):
                source = pool.at[plan_ref[row, m * MAXP + j]]
                slot = target.at[pl.ds(MAXP * j, MAXP), m, part]
                copy = pltpu.make_async_copy(source, slot, sem.at[len(loads)])
                copy.start()
                loads.append(copy)
    return loads


def send_kernel(slots, plan_ref, keys_ref, values_ref, whole_ref, out_ref, held, in_sem, out_sem):
    pools = (keys_ref, values_ref)
    count = 2 * MAXP * slots
    loads = load_pages(plan_ref, 2, slots, pools, held, in_sem.at[pl.ds(0, count)])
    wholes = load_pages(plan_ref, 4, WHOLE, pools, whole_ref, in_sem.at[pl.ds(count, 2 * MAXP * WHOLE)])
    sends = []
    for j in range(MAXP):
        for copy in loads[2 * slots * j : 2 * slots * (j + 1)]:
            copy.wait()
        block = pl.ds(MAXP * j, MAXP)
        send = pltpu.make_async_copy(held.at[block], out_ref.at[block], out_sem.at[j])
        send.start()
        sends.append(send)
    for copy in wholes + sends:
        copy.wait()


def outgoing(plan, keys, values, slots):
    held = (SPREAD, slots, 2, PR, HD)
    return pl.pallas_call(
        functools.partial(send_kernel, slots),
        out_shape=(
            jax.ShapeDtypeStruct((SPREAD, WHOLE, 2, PR, HD), jnp.bfloat16),
            jax.ShapeDtypeStruct(held, jnp.bfloat16),
        ),
        in_specs=[spec(SMEM)] + [spec(pl.ANY)] * 2,
        out_specs=(spec(VMEM), spec(HBM)),
        scratch_shapes=[
            pltpu.VMEM(held, jnp.bfloat16),
            pltpu.SemaphoreType.DMA((2 * MAXP * (slots + WHOLE),)),
            pltpu.SemaphoreType.DMA((MAXP,)),
        ],
        compiler_params=ALONE,
        cost_estimate=cost(6_000_000),
    )(plan, *(pool.reshape(POOL, MAXP, PR, HD) for pool in (keys, values)))


def touch_kernel(*refs):
    refs[-1][...] = jnp.zeros_like(refs[-1])


def touch(array, *through):
    kept = [jax.ShapeDtypeStruct(a.shape, a.dtype) for a in through]
    return pl.pallas_call(
        touch_kernel,
        out_shape=tuple(kept) + (jax.ShapeDtypeStruct((8, HD), jnp.float32),),
        in_specs=[spec(pl.ANY)] * (1 + len(kept)),
        out_specs=(spec(pl.ANY),) * len(kept) + (spec(VMEM),),
        input_output_aliases={1 + i: i for i in range(len(kept))},
        cost_estimate=cost(FILLER),
    )(array, *through)


def cross_kernel(cap, plan_ref, held_ref, *refs):
    keys_ref, values_ref = refs[-2:]

    @pl.loop(0, cap, step=4)
    def _(base):
        for i in range(4):
            place = plan_ref[0, base + i]
            keys_ref[base + i] = held_ref[place, 0]
            values_ref[base + i] = held_ref[place, 1]


def crossing(plan, held, cap, through, after):
    piece = jax.ShapeDtypeStruct((cap, PR, HD), jnp.bfloat16)
    return pl.pallas_call(
        functools.partial(cross_kernel, cap),
        out_shape=(jax.ShapeDtypeStruct(through.shape, through.dtype), piece, piece),
        in_specs=[spec(SMEM), spec(VMEM), spec(pl.ANY), spec(pl.ANY)],
        out_specs=(spec(pl.ANY), spec(VMEM), spec(VMEM)),
        input_output_aliases={2: 0},
        compiler_params=ALONE,
        cost_estimate=cost(4_000_000),
    )(plan, held, through, after)


def deliver_kernel(slots, part, plan_ref, rest_ref, direct_ref, later_ref, *refs):
    out_ref, gathered, ordered, in_sem, out_sem = refs[-5:]
    kept = SPREAD * slots
    crossed = kept + SPREAD * WHOLE
    moves = [
        (rest_ref.at[:, part], gathered.at[0:kept]),
        (direct_ref.at[:, part], gathered.at[kept:crossed]),
        (later_ref, gathered.at[crossed:]),
    ]
    copies = [pltpu.make_async_copy(a, b, in_sem.at[i]) for i, (a, b) in enumerate(moves)]
    for copy in copies:
        copy.start()
    for copy in copies:
        copy.wait()
    step = PIECES // 4
    sends = []
    for quarter in range(4):
        first = quarter * step

        @pl.loop(first, first + step, step=4)
        def _(base):
            for i in range(4):
                ordered[base + i] = gathered[plan_ref[1, base + i]]

        block = pl.ds(first, step)
        send = pltpu.make_async_copy(ordered.at[block], out_ref.at[block], out_sem.at[quarter])
        send.start()
        sends.append(send)
    for send in sends:
        send.wait()


def deliver(plan, rest, direct, later, part, beside, *after):
    slots, cap = rest.shape[0] // SPREAD, later.shape[0]
    return pl.pallas_call(
        functools.partial(deliver_kernel, slots, part),
        out_shape=jax.ShapeDtypeStruct((PIECES, PR, HD), jnp.bfloat16),
        in_specs=[spec(SMEM)] + [spec(pl.ANY)] * (3 + len(after)),
        out_specs=spec(HBM),
        scratch_shapes=[
            pltpu.VMEM((SPREAD * (slots + WHOLE) + cap, PR, HD), jnp.bfloat16),
            pltpu.VMEM((PIECES, PR, HD), jnp.bfloat16),
            pltpu.SemaphoreType.DMA((3,)),
            pltpu.SemaphoreType.DMA((4,)),
        ],
        compiler_params=ALONE,
        cost_estimate=cost(beside),
    )(plan, rest, direct, later, *after)


def place_pages(plan_ref, pool_ref, received_ref, out_ref):
    out_ref[...] = pool_ref[...]

    @pl.loop(0, MOVES)
    def _(k):
        for j in range(MAXP):
            page = plan_ref[3, k * MAXP + j]
            for quarter in range(MAXP):
                first = quarter * PR
                out_ref[page, first : first + PR, :] = received_ref[MAXP * j + quarter, k]


def keys_kernel(own_ref, plan_ref, table_ref, lengths_ref, pool_ref, received_ref, values_ref, *refs):
    blocks, (moved_ref, cache_ref, known_ref, qkv) = refs[:TP], refs[TP:]
    place_pages(plan_ref, pool_ref, received_ref, moved_ref)
    scale = 1.0 / math.sqrt(HD)
    position = lax.broadcasted_iota(jnp.int32, (16, MAXP * PAGE), 1)
    fresh_index = lax.broadcasted_iota(jnp.int32, (16, 16), 1)
    step = lax.broadcasted_iota(jnp.int32, (16, 16), 0) & 1
    by_rows = (((1,), (1,)), ((), ()))
    first_row = (own_ref[0] >> 3) * ROWS
    place = own_ref[0] & (TP - 1)
    for k in range(TP):
        qkv[pl.ds((place ^ k) * 2, 2)] = blocks[k][...]

    def attend(r):
        queries = qkv[r, 0:16, :]
        scores = jnp.concatenate(
            [
                lax.dot_general(
                    queries,
                    moved_ref[table_ref[j, r]],
                    by_rows,
                    preferred_element_type=jnp.float32,
                )
                for j in range(MAXP)
            ],
            axis=1,
        )
        scores = jnp.where(position < lengths_ref[first_row + r], scores * scale, -jnp.inf)
        fresh = lax.dot_general(
            queries, qkv[r, 16:32, :], by_rows, preferred_element_type=jnp.float32
        )
        fresh = jnp.where(fresh_index <= step, fresh * scale, -jnp.inf)
        top = jnp.maximum(
            jnp.max(scores, axis=1, keepdims=True), jnp.max(fresh, axis=1, keepdims=True)
        )
        scores = jnp.exp(scores - top)
        fresh = jnp.exp(fresh - top)
        total = jnp.sum(scores, axis=1, keepdims=True) + jnp.sum(fresh, axis=1, keepdims=True)
        weights = (scores / total).astype(jnp.bfloat16)
        cache_ref[r] = weights
        fresh = (fresh / total).astype(jnp.bfloat16).astype(jnp.float32)
        values = qkv[r, 32:48, :].astype(jnp.float32)
        known = fresh[:, 0:1] * values[0:1, :] + fresh[:, 1:2] * values[1:2, :]
        cached = sum(
            jnp.dot(
                weights[:, j * PAGE : (j + 1) * PAGE],
                values_ref[table_ref[j, r]],
                preferred_element_type=jnp.float32,
            )
            for j in range(MAXP)
        )
        known_ref[r] = known + jnp.where(plan_ref[6, r] < 0, cached, 0.0)

    @pl.loop(0, ROWS, step=4)
    def _(base):
        for i in range(4):
            attend(base + i)


def keys_step(own, plan, table, lengths, pool, received, values, blocks):
    return pl.pallas_call(
        keys_kernel,
        out_shape=(
            jax.ShapeDtypeStruct((POOL, PAGE, HD), jnp.bfloat16),
            jax.ShapeDtypeStruct((ROWS, 16, MAXP * PAGE), jnp.bfloat16),
            jax.ShapeDtypeStruct((ROWS, 16, HD), jnp.float32),
        ),
        in_specs=[spec(SMEM)] * 4 + [spec(VMEM)] * (3 + TP),
        out_specs=(spec(VMEM),) * 3,
        scratch_shapes=[pltpu.VMEM((ROWS, QKV, HD), jnp.bfloat16)],
        compiler_params=LIMIT,
        cost_estimate=cost(FILLER),
    )(own, plan, table, lengths, pool, received, values, *blocks)


def values_kernel(plan_ref, cache_ref, known_ref, received_ref, out_ref, mixed):
    mixed[...] = known_ref[...]
    for k in range(MOVES):
        r = plan_ref[5, k * MAXP]
        values = received_ref[:, k].reshape(MAXP * PAGE, HD)
        mixed[r] = known_ref[r] + jnp.dot(
            cache_ref[r], values, preferred_element_type=jnp.float32
        )
    for r in range(ROWS):
        row = mixed[r]
        for g in range(GROUP):
            head = row[2 * g : 2 * g + 2, :].astype(jnp.bfloat16)
            out_ref[r, :, g * HD : (g + 1) * HD] = head


def values_step(plan, weights, known, received):
    return pl.pallas_call(
        values_kernel,
        out_shape=jax.ShapeDtypeStruct((ROWS, 2, GROUP * HD), jnp.bfloat16),
        in_specs=[spec(SMEM)] + [spec(VMEM)] * 3,
        out_specs=spec(VMEM),
        scratch_shapes=[pltpu.VMEM((ROWS, 16, HD), jnp.float32)],
        compiler_params=LIMIT,
        cost_estimate=cost(4_000_000),
    )(plan, weights, known, received)


def place_step(plan, pool, received):
    return pl.pallas_call(
        place_pages,
        out_shape=jax.ShapeDtypeStruct((POOL, PAGE, HD), jnp.bfloat16),
        in_specs=[spec(SMEM)] + [spec(VMEM)] * 2,
        out_specs=spec(VMEM),
        compiler_params=LIMIT,
        cost_estimate=cost(8_000_000),
    )(plan, pool, received)


def swap(array, axes):
    return lax.all_to_all(array, axes, split_axis=0, concat_axis=0, tiled=True)


def cross(array):
    return lax.ppermute(array, "zh", [(0, 1), (1, 0)])


def move_and_attend(
    slots, cap, own, plan, table, lengths, new_queries, new_keys, new_values, key_pool, value_pool
):
    direct, send = outgoing(plan, key_pool, value_pool, slots)
    direct = cross(direct)
    held = swap(send, ("y", "x")).reshape(SPREAD * slots, 2, PR, HD)
    direct, leaving_keys, leaving_values = crossing(plan, held, cap, direct, *touch(direct))
    later_keys = cross(leaving_keys)
    leaving_values, token = touch(later_keys, leaving_values)
    later_values = cross(leaving_values)
    direct = swap(direct, ("y", "x")).reshape(SPREAD * WHOLE, 2, PR, HD)
    final_keys = deliver(plan, held, direct, later_keys, 0, 4_000_000, token)
    received_keys = swap(final_keys.reshape(SPREAD, MOVES, PR, HD), ("y", "x"))
    final_values = deliver(plan, held, direct, later_values, 1, FILLER)
    blocks = list(pack(own, new_queries, new_keys, new_values, final_values))
    for k in range(1, TP):
        blocks[k] = lax.ppermute(blocks[k], ("zl", "c"), [(i, i ^ k) for i in range(TP)])
    received_values = swap(final_values.reshape(SPREAD, MOVES, PR, HD), ("y", "x"))
    key_moved, weights, known = keys_step(
        own, plan, table, lengths, key_pool, received_keys, value_pool, blocks
    )
    return key_moved, weights, known, received_values


def body(
    new_queries,
    new_keys,
    new_values,
    key_pool,
    value_pool,
    lengths,
    page_table,
    mig_row,
    mig_source,
    mig_pages,
):
    own = lax.axis_index(("y", "zh", "x", "zl", "c")).astype(jnp.int32).reshape(1)
    plan, branch = make_plan(own, mig_row, mig_source, mig_pages, page_table)
    key_moved, weights, known, received_values = lax.switch(
        branch[0],
        [functools.partial(move_and_attend, slots, cap) for slots, cap in BRANCHES],
        own,
        plan,
        page_table.T,
        lengths,
        new_queries,
        new_keys,
        new_values,
        key_pool,
        value_pool,
    )
    mixed = values_step(plan, weights, known, received_values)
    attention = lax.all_to_all(mixed, ("zl", "c"), split_axis=0, concat_axis=2, tiled=True)
    value_moved = place_step(plan, value_pool, received_values)
    return (attention, key_moved, value_moved)


def solution(mesh):
    fine = Mesh(mesh.devices.reshape(4, NZ, NX, 4, 2), ("y", "zh", "x", "zl", "c"))
    inst, tp = ("y", "zh", "x"), ("zl", "c")
    rows = P(inst + tp, None, None)
    pool = P(inst, None, tp)
    return jax.shard_map(
        body,
        mesh=fine,
        in_specs=(rows, rows, rows, pool, pool, P(), P(inst, None), P(), P(), P()),
        out_specs=(rows, pool, pool),
        check_vma=False,
    )
```

```python
import functools
import math

import jax
import jax.numpy as jnp
from jax import lax
from jax.experimental import pallas as pl
from jax.experimental.pallas import tpu as pltpu
from jax.sharding import Mesh
from jax.sharding import PartitionSpec as P

HD = 128
PAGE = 128
MAXP = 4
ROWS = 16
POOL = 64
MOVES = 11
MIGS = 352
NX = 4
NZ = 2
TP = 8
GROUP = 8
SPREAD = 16
PIECES = SPREAD * MOVES
WIDTH = 256
WHOLE = 3
BRANCHES = ((MOVES, SPREAD * (MOVES - WHOLE)), (MOVES - 2, 52), (MOVES - 3, 48))
PR = PAGE * MAXP // SPREAD
QKV = 48
VMEM = pltpu.VMEM
SMEM = pltpu.SMEM
HBM = pltpu.HBM
FILLER = 100_000_000_000
LIMIT = pltpu.CompilerParams(vmem_limit_bytes=40 * 1024 * 1024)
ROOM = pltpu.CompilerParams(vmem_limit_bytes=62_300_000)
ALONE = pltpu.CompilerParams(vmem_limit_bytes=63_400_000)


def spec(space):
    return pl.BlockSpec(memory_space=space)


def cost(bytes_accessed):
    return pl.CostEstimate(flops=100 * bytes_accessed, bytes_accessed=bytes_accessed, transcendentals=0)


def place_of(inst):
    half = (inst >> 2) & 1
    place = ((inst >> 3) << 2) | (inst & 3)
    return half, place


def plan_kernel(own_ref, row_ref, src_ref, pages_ref, table_ref, out_ref, branch_ref):
    own = own_ref[0] >> 3
    half, _ = place_of(own)
    sub = lax.broadcasted_iota(jnp.int32, (MIGS, MIGS), 0)
    lane = lax.broadcasted_iota(jnp.int32, (MIGS, MIGS), 1)

    def to_column(row):
        spread = jnp.where(sub == lane, row.astype(jnp.float32), 0.0)
        return jnp.sum(spread, axis=1, keepdims=True).astype(jnp.int32)

    def to_row(column):
        spread = jnp.where(sub == lane, column.astype(jnp.float32), 0.0)
        return jnp.sum(spread, axis=0, keepdims=True).astype(jnp.int32)

    def count(same):
        return jnp.sum(jnp.where(same, 1.0, 0.0), axis=1, keepdims=True).astype(jnp.int32)

    row_r = row_ref[...].reshape(1, MIGS)
    src_r = src_ref[...].reshape(1, MIGS)
    row_c, src_c = to_column(row_r), to_column(src_r)
    tgt_r, tgt_c = row_r >> 4, row_c >> 4
    sh_r, _ = place_of(src_r)
    th_r, _ = place_of(tgt_r)
    sh_c, sp_c = place_of(src_c)
    th_c, tp_c = place_of(tgt_c)
    before = lane < sub
    same_src = src_c == src_r
    crosses = sh_r != th_r
    rank_src = count(before & same_src)
    rank_tgt = count(before & (tgt_c == tgt_r))
    rank_out = count(before & same_src & crosses)
    fewest = jnp.min(count(same_src & crosses), axis=0, keepdims=True)
    crosses_c = sh_c != th_c
    direct = crosses_c & (rank_out < WHOLE)
    later = crosses_c & (rank_out >= WHOLE)
    needed = jnp.zeros((1, 1), jnp.float32)
    for side in range(NZ):
        leaving = jnp.where(later & (sh_c == side), 1.0, 0.0)
        needed = jnp.maximum(needed, jnp.sum(leaving, axis=0, keepdims=True))
    needed = needed.astype(jnp.int32)
    branch = jnp.zeros((1, 1), jnp.int32)
    slots = jnp.full((1, 1), BRANCHES[0][0], jnp.int32)
    for index, (slots_i, cap) in enumerate(BRANCHES):
        fits = (jnp.minimum(fewest, WHOLE) >= MOVES - slots_i) & (needed <= cap)
        branch = jnp.where(fits, index, branch)
        slots = jnp.where(fits, slots_i, slots)
    rank_rest = rank_src - jnp.minimum(rank_out, WHOLE)
    later_r = to_row(jnp.where(later, 1, 0)) > 0
    rank_later = count(before & later_r & (sh_c == sh_r))
    rest_place = sp_c * slots + rank_rest
    direct_place = SPREAD * slots + sp_c * WHOLE + rank_out
    origin = jnp.where(sh_c == th_c, rest_place, SPREAD * (slots + WHOLE) + rank_later)
    origin = jnp.where(direct, direct_place, origin)
    final_place = tp_c * MOVES + rank_tgt
    col = lax.broadcasted_iota(jnp.int32, (1, WIDTH), 1)
    message, page = col >> 2, col & 3

    def pick(chosen, value):
        picked = jnp.where(chosen, value.astype(jnp.float32), 0.0)
        return jnp.sum(picked, axis=0, keepdims=True).astype(jnp.int32)

    def by_page(pages):
        chosen = pages[MAXP - 1]
        for j in range(MAXP - 1):
            chosen = jnp.where(page == j, pages[j], chosen)
        return chosen

    out_ref[0:1, :] = pick(later & (sh_c == half) & (rank_later == col), rest_place)
    out_ref[1:2, :] = pick((th_c == half) & (final_place == col), origin)
    pages = by_page([to_column(pages_ref[j : j + 1, :]) for j in range(MAXP)])
    mine = src_c == own
    out_ref[2:3, :] = pick(mine & ~direct & (rank_rest == message), pages)
    arrival = pick((tgt_c == own) & (rank_tgt == message), row_c & (ROWS - 1))
    sub16 = lax.broadcasted_iota(jnp.int32, (ROWS, ROWS), 0)
    lane16 = lax.broadcasted_iota(jnp.int32, (ROWS, ROWS), 1)

    def table_column(j):
        spread = jnp.where(sub16 == lane16, table_ref[j : j + 1, :].astype(jnp.float32), 0.0)
        return jnp.sum(spread, axis=1, keepdims=True).astype(jnp.int32)

    table = by_page([table_column(j) for j in range(MAXP)])
    row_id = lax.broadcasted_iota(jnp.int32, (ROWS, WIDTH), 0)
    out_ref[3:4, :] = pick(row_id == arrival, table)
    out_ref[4:5, :] = pick(mine & direct & (rank_out == message), pages)
    out_ref[5:6, :] = arrival
    branch_ref[0] = branch[0, 0]
    out_ref[6:7, :] = pick((tgt_c == own) & ((row_c & (ROWS - 1)) == col), rank_tgt + 1) - 1
    out_ref[7:8, :] = jnp.zeros((1, WIDTH), jnp.int32)


def make_plan(own, mig_row, mig_source, mig_pages, page_table):
    return pl.pallas_call(
        plan_kernel,
        out_shape=(
            jax.ShapeDtypeStruct((8, WIDTH), jnp.int32),
            jax.ShapeDtypeStruct((1,), jnp.int32),
        ),
        in_specs=[spec(SMEM), spec(VMEM), spec(VMEM), spec(VMEM), spec(VMEM)],
        out_specs=(spec(VMEM), spec(SMEM)),
        compiler_params=ALONE,
        cost_estimate=cost(100_000),
    )(own, mig_row, mig_source, mig_pages.T, page_table.T)


def pack_kernel(own_ref, q_ref, k_ref, v_ref, after_ref, *refs):
    blocks, scratch = refs[:TP], refs[TP]
    scratch[...] = jnp.zeros_like(scratch)
    place = own_ref[0] & (TP - 1)

    @pl.loop(0, TP)
    def _(k):
        d = place ^ k
        own_head = pl.ds(pl.multiple_of(d * HD, HD), HD)
        for r in range(2):
            for g in range(GROUP):
                head = pl.ds(pl.multiple_of((d * GROUP + g) * HD, HD), HD)
                scratch[k, r, 2 * g : 2 * g + 2, :] = q_ref[r, :, head].astype(jnp.float32)
            scratch[k, r, 16:18, :] = k_ref[r, :, own_head].astype(jnp.float32)
            scratch[k, r, 32:34, :] = v_ref[r, :, own_head].astype(jnp.float32)

    for k in range(TP):
        blocks[k][...] = scratch[k].astype(jnp.bfloat16)


def pack(own, new_queries, new_keys, new_values, after):
    return pl.pallas_call(
        pack_kernel,
        out_shape=(jax.ShapeDtypeStruct((2, QKV, HD), jnp.bfloat16),) * TP,
        in_specs=[spec(SMEM)] + [spec(VMEM)] * 3 + [spec(pl.ANY)],
        out_specs=(spec(VMEM),) * TP,
        scratch_shapes=[pltpu.VMEM((TP, 2, QKV, HD), jnp.float32)],
        compiler_params=LIMIT,
        cost_estimate=cost(400_000),
    )(own, new_queries, new_keys, new_values, after)


def send_kernel(slots, plan_ref, keys_ref, values_ref, whole_ref, out_ref, held, in_sem, out_sem):
    def load(row, messages, target, j, sem):
        for m in range(messages):
            for part, pool in enumerate((keys_ref, values_ref)):
                source = pool.at[plan_ref[row, m * MAXP + j]]
                slot = target.at[pl.ds(MAXP * j, MAXP), m, part]
                pltpu.make_async_copy(source, slot, sem).start()

    def wait(target, sem):
        pltpu.make_async_copy(target, target, sem).wait()

    for j in range(MAXP):
        load(4, WHOLE, whole_ref, j, in_sem.at[MAXP])
    for j in range(MAXP):
        load(2, slots, held, j, in_sem.at[j])
    sends = []
    for j in range(MAXP):
        block = pl.ds(MAXP * j, MAXP)
        wait(held.at[block], in_sem.at[j])
        send = pltpu.make_async_copy(held.at[block], out_ref.at[block], out_sem.at[j])
        send.start()
        sends.append(send)
    wait(whole_ref, in_sem.at[MAXP])
    for send in sends:
        send.wait()


def outgoing(plan, keys, values, slots):
    held = (SPREAD, slots, 2, PR, HD)
    return pl.pallas_call(
        functools.partial(send_kernel, slots),
        out_shape=(
            jax.ShapeDtypeStruct((SPREAD, WHOLE, 2, PR, HD), jnp.bfloat16),
            jax.ShapeDtypeStruct(held, jnp.bfloat16),
        ),
        in_specs=[spec(SMEM)] + [spec(pl.ANY)] * 2,
        out_specs=(spec(VMEM), spec(HBM)),
        scratch_shapes=[
            pltpu.VMEM(held, jnp.bfloat16),
            pltpu.SemaphoreType.DMA((MAXP + 1,)),
            pltpu.SemaphoreType.DMA((MAXP,)),
        ],
        compiler_params=ROOM,
        cost_estimate=cost(6_000_000),
    )(plan, *(pool.reshape(POOL, MAXP, PR, HD) for pool in (keys, values)))


def touch_kernel(*refs):
    refs[-1][...] = jnp.zeros_like(refs[-1])


def touch(array, *through):
    kept = [jax.ShapeDtypeStruct(a.shape, a.dtype) for a in through]
    return pl.pallas_call(
        touch_kernel,
        out_shape=tuple(kept) + (jax.ShapeDtypeStruct((8, HD), jnp.float32),),
        in_specs=[spec(pl.ANY)] * (1 + len(kept)),
        out_specs=(spec(pl.ANY),) * len(kept) + (spec(VMEM),),
        input_output_aliases={1 + i: i for i in range(len(kept))},
        cost_estimate=cost(FILLER),
    )(array, *through)


def cross_kernel(cap, plan_ref, held_ref, *refs):
    keys_ref, values_ref = refs[-2:]

    @pl.loop(0, cap, step=4)
    def _(base):
        for i in range(4):
            place = plan_ref[0, base + i]
            keys_ref[base + i] = held_ref[place, 0]
            values_ref[base + i] = held_ref[place, 1]


def crossing(plan, held, cap, through, after):
    piece = jax.ShapeDtypeStruct((cap, PR, HD), jnp.bfloat16)
    return pl.pallas_call(
        functools.partial(cross_kernel, cap),
        out_shape=(jax.ShapeDtypeStruct(through.shape, through.dtype), piece, piece),
        in_specs=[spec(SMEM), spec(VMEM), spec(pl.ANY), spec(pl.ANY)],
        out_specs=(spec(pl.ANY), spec(VMEM), spec(VMEM)),
        input_output_aliases={2: 0},
        compiler_params=ALONE,
        cost_estimate=cost(4_000_000),
    )(plan, held, through, after)


def deliver_kernel(slots, part, unread, plan_ref, rest_ref, direct_ref, later_ref, *refs):
    gathered, ordered, in_sem, out_sem = refs[-4:]
    out_ref = refs[unread]
    if part:
        refs[unread + 1][...] = jnp.zeros_like(refs[unread + 1])
    kept = SPREAD * slots
    crossed = kept + SPREAD * WHOLE
    moves = [
        (rest_ref.at[:, part], gathered.at[0:kept]),
        (direct_ref.at[:, part], gathered.at[kept:crossed]),
        (later_ref, gathered.at[crossed:]),
    ]
    copies = [pltpu.make_async_copy(a, b, in_sem.at[i]) for i, (a, b) in enumerate(moves)]
    for copy in copies:
        copy.start()
    for copy in copies:
        copy.wait()
    step = PIECES // 4
    sends = []
    for quarter in range(4):
        first = quarter * step

        @pl.loop(first, first + step, step=11)
        def _(base):
            for i in range(11):
                ordered[base + i] = gathered[plan_ref[1, base + i]]

        block = pl.ds(first, step)
        send = pltpu.make_async_copy(ordered.at[block], out_ref.at[block], out_sem.at[quarter])
        send.start()
        sends.append(send)
    for send in sends:
        send.wait()


def deliver(plan, rest, direct, later, part, beside, *after):
    slots, cap = rest.shape[0] // SPREAD, later.shape[0]
    shapes = (
        jax.ShapeDtypeStruct((PIECES, PR, HD), jnp.bfloat16),
        jax.ShapeDtypeStruct((8, HD), jnp.float32),
    )
    return pl.pallas_call(
        functools.partial(deliver_kernel, slots, part, len(after)),
        out_shape=shapes if part else shapes[0],
        in_specs=[spec(SMEM)] + [spec(pl.ANY)] * (3 + len(after)),
        out_specs=(spec(HBM), spec(VMEM)) if part else spec(HBM),
        scratch_shapes=[
            pltpu.VMEM((SPREAD * (slots + WHOLE) + cap, PR, HD), jnp.bfloat16),
            pltpu.VMEM((PIECES, PR, HD), jnp.bfloat16),
            pltpu.SemaphoreType.DMA((3,)),
            pltpu.SemaphoreType.DMA((4,)),
        ],
        compiler_params=ALONE,
        cost_estimate=cost(beside),
    )(plan, rest, direct, later, *after)


def place_pages(plan_ref, received_ref, moved):
    @pl.loop(0, MOVES)
    def _(k):
        for j in range(MAXP):
            page = plan_ref[3, k * MAXP + j]
            for quarter in range(MAXP):
                first = quarter * PR
                moved[page, first : first + PR, :] = received_ref[MAXP * j + quarter, k]


def keys_kernel(own_ref, plan_ref, table_ref, lengths_ref, pool_ref, received_ref, values_ref, *refs):
    blocks, (out_ref, cache_ref, known_ref, moved_ref, sem, qkv, scores, fresh_scores) = refs[:TP], refs[TP:]
    load = pltpu.make_async_copy(pool_ref, moved_ref, sem.at[0])
    store = pltpu.make_async_copy(moved_ref, out_ref, sem.at[1])
    load.start()
    scale = 1.0 / math.sqrt(HD)
    position = lax.broadcasted_iota(jnp.int32, (16, PAGE), 1)
    fresh_index = lax.broadcasted_iota(jnp.int32, (16, 16), 1)
    step = lax.broadcasted_iota(jnp.int32, (16, 16), 0) & 1
    by_rows = (((1,), (1,)), ((), ()))
    first_row = (own_ref[0] >> 3) * ROWS
    place = own_ref[0] & (TP - 1)
    for k in range(TP):
        qkv[pl.ds((place ^ k) * 2, 2)] = blocks[k][...]
    load.wait()
    place_pages(plan_ref, received_ref, moved_ref)
    store.start()

    @pl.loop(0, ROWS, step=4)
    def _(base):
        for i in range(4):
            r = base + i
            queries = qkv[r, 0:16, :]
            length = lengths_ref[first_row + r]
            for j in range(MAXP):
                page = moved_ref[table_ref[j, r]]
                part = lax.dot_general(queries, page, by_rows, preferred_element_type=jnp.float32)
                part = jnp.where(position + j * PAGE < length, part * scale, -jnp.inf)
                scores[r, :, j * PAGE : (j + 1) * PAGE] = part
            part = lax.dot_general(
                queries, qkv[r, 16:32, :], by_rows, preferred_element_type=jnp.float32
            )
            fresh_scores[r] = jnp.where(fresh_index <= step, part * scale, -jnp.inf)

    @pl.loop(0, ROWS, step=4)
    def _(base):
        rows = pl.ds(base, 4)
        cache, fresh = scores[rows], fresh_scores[rows]
        top = jnp.maximum(
            jnp.max(cache, axis=-1, keepdims=True), jnp.max(fresh, axis=-1, keepdims=True)
        )
        cache, fresh = jnp.exp(cache - top), jnp.exp(fresh - top)
        total = jnp.sum(cache, axis=-1, keepdims=True) + jnp.sum(fresh, axis=-1, keepdims=True)
        cache_ref[rows] = (cache / total).astype(jnp.bfloat16)
        fresh = (fresh / total).astype(jnp.bfloat16).astype(jnp.float32)
        values = qkv[rows, 32:48, :].astype(jnp.float32)
        known_ref[rows] = fresh[:, :, 0:1] * values[:, 0:1, :] + fresh[:, :, 1:2] * values[:, 1:2, :]

    @pl.loop(0, ROWS)
    def _(r):
        @pl.when(plan_ref[6, r] < 0)
        def _():
            cached = jnp.zeros((16, HD), jnp.float32)
            for j in range(MAXP):
                weights = cache_ref[r, :, j * PAGE : (j + 1) * PAGE]
                page = values_ref[table_ref[j, r]]
                cached += jnp.dot(weights, page, preferred_element_type=jnp.float32)
            known_ref[r] += cached

    store.wait()


def keys_step(own, plan, table, lengths, pool, received, values, blocks):
    return pl.pallas_call(
        keys_kernel,
        out_shape=(
            jax.ShapeDtypeStruct((POOL, PAGE, HD), jnp.bfloat16),
            jax.ShapeDtypeStruct((ROWS, 16, MAXP * PAGE), jnp.bfloat16),
            jax.ShapeDtypeStruct((ROWS, 16, HD), jnp.float32),
        ),
        in_specs=[spec(SMEM)] * 4 + [spec(pl.ANY)] + [spec(VMEM)] * (2 + TP),
        out_specs=(spec(pl.ANY), spec(VMEM), spec(VMEM)),
        scratch_shapes=[
            pltpu.VMEM((POOL, PAGE, HD), jnp.bfloat16),
            pltpu.SemaphoreType.DMA((2,)),
            pltpu.VMEM((ROWS, QKV, HD), jnp.bfloat16),
            pltpu.VMEM((ROWS, 16, MAXP * PAGE), jnp.float32),
            pltpu.VMEM((ROWS, 16, 16), jnp.float32),
        ],
        compiler_params=LIMIT,
        cost_estimate=cost(8_000_000),
    )(own, plan, table, lengths, pool, received, values, *blocks)


def values_kernel(plan_ref, cache_ref, known_ref, received_ref, out_ref, mixed):
    mixed[...] = known_ref[...]
    for k in range(MOVES):
        r = plan_ref[5, k * MAXP]
        values = received_ref[:, k].reshape(MAXP * PAGE, HD)
        mixed[r] = known_ref[r] + jnp.dot(
            cache_ref[r], values, preferred_element_type=jnp.float32
        )
    for r in range(ROWS):
        row = mixed[r]
        for g in range(GROUP):
            head = row[2 * g : 2 * g + 2, :].astype(jnp.bfloat16)
            out_ref[r, :, g * HD : (g + 1) * HD] = head


def values_step(plan, weights, known, received):
    return pl.pallas_call(
        values_kernel,
        out_shape=jax.ShapeDtypeStruct((ROWS, 2, GROUP * HD), jnp.bfloat16),
        in_specs=[spec(SMEM)] + [spec(VMEM)] * 3,
        out_specs=spec(VMEM),
        scratch_shapes=[pltpu.VMEM((ROWS, 16, HD), jnp.float32)],
        compiler_params=LIMIT,
        cost_estimate=cost(4_000_000),
    )(plan, weights, known, received)


def place_kernel(plan_ref, pool_ref, received_ref, out_ref, moved, arrived, sem):
    pairs = [(pool_ref, moved), (received_ref, arrived)]
    loads = [pltpu.make_async_copy(a, b, sem.at[i]) for i, (a, b) in enumerate(pairs)]
    store = pltpu.make_async_copy(moved, out_ref, sem.at[2])
    for load in loads:
        load.start()
    for load in loads:
        load.wait()
    place_pages(plan_ref, arrived, moved)
    store.start()
    store.wait()


def place_step(plan, pool, received):
    return pl.pallas_call(
        place_kernel,
        out_shape=jax.ShapeDtypeStruct((POOL, PAGE, HD), jnp.bfloat16),
        in_specs=[spec(SMEM), spec(pl.ANY), spec(pl.ANY)],
        out_specs=spec(pl.ANY),
        scratch_shapes=[
            pltpu.VMEM((POOL, PAGE, HD), jnp.bfloat16),
            pltpu.VMEM((SPREAD, MOVES, PR, HD), jnp.bfloat16),
            pltpu.SemaphoreType.DMA((3,)),
        ],
        compiler_params=LIMIT,
        cost_estimate=cost(8_000_000),
    )(plan, pool, received)


def swap(array, axes):
    return lax.all_to_all(array, axes, split_axis=0, concat_axis=0, tiled=True)


def cross(array):
    return lax.ppermute(array, "zh", [(0, 1), (1, 0)])


def move_and_attend(
    slots, cap, own, plan, table, lengths, new_queries, new_keys, new_values, key_pool, value_pool
):
    direct, send = outgoing(plan, key_pool, value_pool, slots)
    direct = cross(direct)
    held = swap(send, ("y", "x")).reshape(SPREAD * slots, 2, PR, HD)
    direct, leaving_keys, leaving_values = crossing(plan, held, cap, direct, *touch(direct))
    later_keys = cross(leaving_keys)
    leaving_values, token = touch(later_keys, leaving_values)
    later_values = cross(leaving_values)
    direct = swap(direct, ("y", "x")).reshape(SPREAD * WHOLE, 2, PR, HD)
    final_keys = deliver(plan, held, direct, later_keys, 0, 4_000_000, token)
    received_keys = swap(final_keys.reshape(SPREAD, MOVES, PR, HD), ("y", "x"))
    final_values, token = deliver(plan, held, direct, later_values, 1, FILLER)
    blocks = list(pack(own, new_queries, new_keys, new_values, token))
    for k in range(1, TP):
        blocks[k] = lax.ppermute(blocks[k], ("zl", "c"), [(i, i ^ k) for i in range(TP)])
    received_values = swap(final_values.reshape(SPREAD, MOVES, PR, HD), ("y", "x"))
    key_moved, weights, known = keys_step(
        own, plan, table, lengths, key_pool, received_keys, value_pool, blocks
    )
    return key_moved, weights, known, received_values


def body(
    new_queries,
    new_keys,
    new_values,
    key_pool,
    value_pool,
    lengths,
    page_table,
    mig_row,
    mig_source,
    mig_pages,
):
    own = lax.axis_index(("y", "zh", "x", "zl", "c")).astype(jnp.int32).reshape(1)
    plan, branch = make_plan(own, mig_row, mig_source, mig_pages, page_table)
    key_moved, weights, known, received_values = lax.switch(
        branch[0],
        [functools.partial(move_and_attend, slots, cap) for slots, cap in BRANCHES],
        own,
        plan,
        page_table.T,
        lengths,
        new_queries,
        new_keys,
        new_values,
        key_pool,
        value_pool,
    )
    mixed = values_step(plan, weights, known, received_values)
    attention = lax.all_to_all(mixed, ("zl", "c"), split_axis=0, concat_axis=2, tiled=True)
    value_moved = place_step(plan, value_pool, received_values)
    return (attention, key_moved, value_moved)


def solution(mesh):
    fine = Mesh(mesh.devices.reshape(4, NZ, NX, 4, 2), ("y", "zh", "x", "zl", "c"))
    inst, tp = ("y", "zh", "x"), ("zl", "c")
    rows = P(inst + tp, None, None)
    pool = P(inst, None, tp)
    return jax.shard_map(
        body,
        mesh=fine,
        in_specs=(rows, rows, rows, pool, pool, P(), P(inst, None), P(), P(), P()),
        out_specs=(rows, pool, pool),
        check_vma=False,
    )
```

```python
import functools
import math

import jax
import jax.numpy as jnp
from jax import lax
from jax.experimental import pallas as pl
from jax.experimental.pallas import tpu as pltpu
from jax.sharding import Mesh
from jax.sharding import PartitionSpec as P

HD = 128
PAGE = 128
MAXP = 4
ROWS = 16
POOL = 64
MOVES = 11
MIGS = 352
NX = 4
NZ = 2
TP = 8
GROUP = 8
SPREAD = 16
PIECES = SPREAD * MOVES
WIDTH = 256
WHOLE = 3
BRANCHES = ((MOVES, SPREAD * (MOVES - WHOLE)), (MOVES - 2, 52), (MOVES - 3, 48))
PR = PAGE * MAXP // SPREAD
QKV = 48
VMEM = pltpu.VMEM
SMEM = pltpu.SMEM
HBM = pltpu.HBM
FILLER = 100_000_000_000
LIMIT = pltpu.CompilerParams(vmem_limit_bytes=40 * 1024 * 1024)
ROOM = pltpu.CompilerParams(vmem_limit_bytes=62_300_000)
ALONE = pltpu.CompilerParams(vmem_limit_bytes=63_400_000)


def spec(space):
    return pl.BlockSpec(memory_space=space)


def cost(bytes_accessed):
    return pl.CostEstimate(flops=100 * bytes_accessed, bytes_accessed=bytes_accessed, transcendentals=0)


def place_of(inst):
    half = (inst >> 2) & 1
    place = ((inst >> 3) << 2) | (inst & 3)
    return half, place


def plan_kernel(own_ref, row_ref, src_ref, pages_ref, table_ref, out_ref, branch_ref):
    own = own_ref[0] >> 3
    half, _ = place_of(own)
    sub = lax.broadcasted_iota(jnp.int32, (MIGS, MIGS), 0)
    lane = lax.broadcasted_iota(jnp.int32, (MIGS, MIGS), 1)

    def to_column(row):
        spread = jnp.where(sub == lane, row.astype(jnp.float32), 0.0)
        return jnp.sum(spread, axis=1, keepdims=True).astype(jnp.int32)

    def to_row(column):
        spread = jnp.where(sub == lane, column.astype(jnp.float32), 0.0)
        return jnp.sum(spread, axis=0, keepdims=True).astype(jnp.int32)

    def count(same):
        return jnp.sum(jnp.where(same, 1.0, 0.0), axis=1, keepdims=True).astype(jnp.int32)

    row_r = row_ref[...].reshape(1, MIGS)
    src_r = src_ref[...].reshape(1, MIGS)
    row_c, src_c = to_column(row_r), to_column(src_r)
    tgt_r, tgt_c = row_r >> 4, row_c >> 4
    sh_r, _ = place_of(src_r)
    th_r, _ = place_of(tgt_r)
    sh_c, sp_c = place_of(src_c)
    th_c, tp_c = place_of(tgt_c)
    before = lane < sub
    same_src = src_c == src_r
    crosses = sh_r != th_r
    rank_src = count(before & same_src)
    rank_tgt = count(before & (tgt_c == tgt_r))
    rank_out = count(before & same_src & crosses)
    fewest = jnp.min(count(same_src & crosses), axis=0, keepdims=True)
    crosses_c = sh_c != th_c
    direct = crosses_c & (rank_out < WHOLE)
    later = crosses_c & (rank_out >= WHOLE)
    needed = jnp.zeros((1, 1), jnp.float32)
    for side in range(NZ):
        leaving = jnp.where(later & (sh_c == side), 1.0, 0.0)
        needed = jnp.maximum(needed, jnp.sum(leaving, axis=0, keepdims=True))
    needed = needed.astype(jnp.int32)
    branch = jnp.zeros((1, 1), jnp.int32)
    slots = jnp.full((1, 1), BRANCHES[0][0], jnp.int32)
    for index, (slots_i, cap) in enumerate(BRANCHES):
        fits = (jnp.minimum(fewest, WHOLE) >= MOVES - slots_i) & (needed <= cap)
        branch = jnp.where(fits, index, branch)
        slots = jnp.where(fits, slots_i, slots)
    rank_rest = rank_src - jnp.minimum(rank_out, WHOLE)
    later_r = to_row(jnp.where(later, 1, 0)) > 0
    rank_later = count(before & later_r & (sh_c == sh_r))
    rest_place = sp_c * slots + rank_rest
    direct_place = SPREAD * slots + sp_c * WHOLE + rank_out
    origin = jnp.where(sh_c == th_c, rest_place, SPREAD * (slots + WHOLE) + rank_later)
    origin = jnp.where(direct, direct_place, origin)
    final_place = tp_c * MOVES + rank_tgt
    col = lax.broadcasted_iota(jnp.int32, (1, WIDTH), 1)
    message, page = col >> 2, col & 3

    def pick(chosen, value):
        picked = jnp.where(chosen, value.astype(jnp.float32), 0.0)
        return jnp.sum(picked, axis=0, keepdims=True).astype(jnp.int32)

    def by_page(pages):
        chosen = pages[MAXP - 1]
        for j in range(MAXP - 1):
            chosen = jnp.where(page == j, pages[j], chosen)
        return chosen

    out_ref[0:1, :] = pick(later & (sh_c == half) & (rank_later == col), rest_place)
    out_ref[1:2, :] = pick((th_c == half) & (final_place == col), origin)
    pages = by_page([to_column(pages_ref[j : j + 1, :]) for j in range(MAXP)])
    mine = src_c == own
    out_ref[2:3, :] = pick(mine & ~direct & (rank_rest == message), pages)
    arrival = pick((tgt_c == own) & (rank_tgt == message), row_c & (ROWS - 1))
    sub16 = lax.broadcasted_iota(jnp.int32, (ROWS, ROWS), 0)
    lane16 = lax.broadcasted_iota(jnp.int32, (ROWS, ROWS), 1)

    def table_column(j):
        spread = jnp.where(sub16 == lane16, table_ref[j : j + 1, :].astype(jnp.float32), 0.0)
        return jnp.sum(spread, axis=1, keepdims=True).astype(jnp.int32)

    table = by_page([table_column(j) for j in range(MAXP)])
    row_id = lax.broadcasted_iota(jnp.int32, (ROWS, WIDTH), 0)
    out_ref[3:4, :] = pick(row_id == arrival, table)
    out_ref[4:5, :] = pick(mine & direct & (rank_out == message), pages)
    out_ref[5:6, :] = arrival
    branch_ref[0] = branch[0, 0]
    out_ref[6:7, :] = pick((tgt_c == own) & ((row_c & (ROWS - 1)) == col), rank_tgt + 1) - 1
    out_ref[7:8, :] = jnp.zeros((1, WIDTH), jnp.int32)


def make_plan(own, mig_row, mig_source, mig_pages, page_table):
    return pl.pallas_call(
        plan_kernel,
        out_shape=(
            jax.ShapeDtypeStruct((8, WIDTH), jnp.int32),
            jax.ShapeDtypeStruct((1,), jnp.int32),
        ),
        in_specs=[spec(SMEM), spec(VMEM), spec(VMEM), spec(VMEM), spec(VMEM)],
        out_specs=(spec(VMEM), spec(SMEM)),
        compiler_params=ALONE,
        cost_estimate=cost(100_000),
    )(own, mig_row, mig_source, mig_pages.T, page_table.T)


def pack_kernel(own_ref, q_ref, k_ref, v_ref, after_ref, *refs):
    blocks, scratch = refs[:TP], refs[TP]
    scratch[...] = jnp.zeros_like(scratch)
    place = own_ref[0] & (TP - 1)

    @pl.loop(0, TP)
    def _(k):
        d = place ^ k
        own_head = pl.ds(pl.multiple_of(d * HD, HD), HD)
        for r in range(2):
            for g in range(GROUP):
                head = pl.ds(pl.multiple_of((d * GROUP + g) * HD, HD), HD)
                scratch[k, r, 2 * g : 2 * g + 2, :] = q_ref[r, :, head].astype(jnp.float32)
            scratch[k, r, 16:18, :] = k_ref[r, :, own_head].astype(jnp.float32)
            scratch[k, r, 32:34, :] = v_ref[r, :, own_head].astype(jnp.float32)

    for k in range(TP):
        blocks[k][...] = scratch[k].astype(jnp.bfloat16)


def pack(own, new_queries, new_keys, new_values, after):
    return pl.pallas_call(
        pack_kernel,
        out_shape=(jax.ShapeDtypeStruct((2, QKV, HD), jnp.bfloat16),) * TP,
        in_specs=[spec(SMEM)] + [spec(VMEM)] * 3 + [spec(pl.ANY)],
        out_specs=(spec(VMEM),) * TP,
        scratch_shapes=[pltpu.VMEM((TP, 2, QKV, HD), jnp.float32)],
        compiler_params=LIMIT,
        cost_estimate=cost(400_000),
    )(own, new_queries, new_keys, new_values, after)


def send_kernel(slots, plan_ref, keys_ref, values_ref, whole_ref, out_ref, held, in_sem, out_sem):
    def load(row, messages, target, j, sem):
        for m in range(messages):
            for part, pool in enumerate((keys_ref, values_ref)):
                source = pool.at[plan_ref[row, m * MAXP + j]]
                slot = target.at[pl.ds(MAXP * j, MAXP), m, part]
                pltpu.make_async_copy(source, slot, sem).start()

    def wait(target, sem):
        pltpu.make_async_copy(target, target, sem).wait()

    for j in range(MAXP):
        load(4, WHOLE, whole_ref, j, in_sem.at[MAXP])
    for j in range(MAXP):
        load(2, slots, held, j, in_sem.at[j])
    sends = []
    for j in range(MAXP):
        block = pl.ds(MAXP * j, MAXP)
        wait(held.at[block], in_sem.at[j])
        send = pltpu.make_async_copy(held.at[block], out_ref.at[block], out_sem.at[j])
        send.start()
        sends.append(send)
    wait(whole_ref, in_sem.at[MAXP])
    for send in sends:
        send.wait()


def outgoing(plan, keys, values, slots):
    held = (SPREAD, slots, 2, PR, HD)
    return pl.pallas_call(
        functools.partial(send_kernel, slots),
        out_shape=(
            jax.ShapeDtypeStruct((SPREAD, WHOLE, 2, PR, HD), jnp.bfloat16),
            jax.ShapeDtypeStruct(held, jnp.bfloat16),
        ),
        in_specs=[spec(SMEM)] + [spec(pl.ANY)] * 2,
        out_specs=(spec(VMEM), spec(HBM)),
        scratch_shapes=[
            pltpu.VMEM(held, jnp.bfloat16),
            pltpu.SemaphoreType.DMA((MAXP + 1,)),
            pltpu.SemaphoreType.DMA((MAXP,)),
        ],
        compiler_params=ROOM,
        cost_estimate=cost(6_000_000),
    )(plan, *(pool.reshape(POOL, MAXP, PR, HD) for pool in (keys, values)))


def touch_kernel(*refs):
    refs[-1][...] = jnp.zeros_like(refs[-1])


def touch(array, *through):
    kept = [jax.ShapeDtypeStruct(a.shape, a.dtype) for a in through]
    return pl.pallas_call(
        touch_kernel,
        out_shape=tuple(kept) + (jax.ShapeDtypeStruct((8, HD), jnp.float32),),
        in_specs=[spec(pl.ANY)] * (1 + len(kept)),
        out_specs=(spec(pl.ANY),) * len(kept) + (spec(VMEM),),
        input_output_aliases={1 + i: i for i in range(len(kept))},
        cost_estimate=cost(FILLER),
    )(array, *through)


def cross_kernel(cap, plan_ref, held_ref, *refs):
    keys_ref, values_ref = refs[-2:]

    @pl.loop(0, cap, step=4)
    def _(base):
        for i in range(4):
            place = plan_ref[0, base + i]
            keys_ref[base + i] = held_ref[place, 0]
            values_ref[base + i] = held_ref[place, 1]


def crossing(plan, held, cap, through, after):
    piece = jax.ShapeDtypeStruct((cap, PR, HD), jnp.bfloat16)
    return pl.pallas_call(
        functools.partial(cross_kernel, cap),
        out_shape=(jax.ShapeDtypeStruct(through.shape, through.dtype), piece, piece),
        in_specs=[spec(SMEM), spec(VMEM), spec(pl.ANY), spec(pl.ANY)],
        out_specs=(spec(pl.ANY), spec(VMEM), spec(VMEM)),
        input_output_aliases={2: 0},
        compiler_params=ALONE,
        cost_estimate=cost(4_000_000),
    )(plan, held, through, after)


def deliver_kernel(slots, part, unread, plan_ref, rest_ref, direct_ref, later_ref, *refs):
    gathered, ordered, in_sem, out_sem = refs[-4:]
    out_ref = refs[unread]
    if part:
        refs[unread + 1][...] = jnp.zeros_like(refs[unread + 1])
    kept = SPREAD * slots
    crossed = kept + SPREAD * WHOLE
    moves = [
        (rest_ref.at[:, part], gathered.at[0:kept]),
        (direct_ref.at[:, part], gathered.at[kept:crossed]),
        (later_ref, gathered.at[crossed:]),
    ]
    copies = [pltpu.make_async_copy(a, b, in_sem.at[i]) for i, (a, b) in enumerate(moves)]
    for copy in copies:
        copy.start()
    for copy in copies:
        copy.wait()
    step = PIECES // 4
    sends = []
    for quarter in range(4):
        first = quarter * step

        @pl.loop(first, first + step, step=11)
        def _(base):
            for i in range(11):
                ordered[base + i] = gathered[plan_ref[1, base + i]]

        block = pl.ds(first, step)
        send = pltpu.make_async_copy(ordered.at[block], out_ref.at[block], out_sem.at[quarter])
        send.start()
        sends.append(send)
    for send in sends:
        send.wait()


def deliver(plan, rest, direct, later, part, beside, *after):
    slots, cap = rest.shape[0] // SPREAD, later.shape[0]
    shapes = (
        jax.ShapeDtypeStruct((PIECES, PR, HD), jnp.bfloat16),
        jax.ShapeDtypeStruct((8, HD), jnp.float32),
    )
    return pl.pallas_call(
        functools.partial(deliver_kernel, slots, part, len(after)),
        out_shape=shapes if part else shapes[0],
        in_specs=[spec(SMEM)] + [spec(pl.ANY)] * (3 + len(after)),
        out_specs=(spec(HBM), spec(VMEM)) if part else spec(HBM),
        scratch_shapes=[
            pltpu.VMEM((SPREAD * (slots + WHOLE) + cap, PR, HD), jnp.bfloat16),
            pltpu.VMEM((PIECES, PR, HD), jnp.bfloat16),
            pltpu.SemaphoreType.DMA((3,)),
            pltpu.SemaphoreType.DMA((4,)),
        ],
        compiler_params=ALONE,
        cost_estimate=cost(beside),
    )(plan, rest, direct, later, *after)


def place_pages(plan_ref, received_ref, moved):
    @pl.loop(0, MOVES)
    def _(k):
        for j in range(MAXP):
            page = plan_ref[3, k * MAXP + j]
            for quarter in range(MAXP):
                first = quarter * PR
                moved[page, first : first + PR, :] = received_ref[MAXP * j + quarter, k]


def keys_kernel(own_ref, plan_ref, table_ref, lengths_ref, pool_ref, received_ref, values_ref, *refs):
    blocks, (out_ref, cache_ref, known_ref, moved_ref, sem, qkv, scores, fresh_scores) = refs[:TP], refs[TP:]
    load = pltpu.make_async_copy(pool_ref, moved_ref, sem.at[0])
    store = pltpu.make_async_copy(moved_ref, out_ref, sem.at[1])
    load.start()
    scale = 1.0 / math.sqrt(HD)
    position = lax.broadcasted_iota(jnp.int32, (16, PAGE), 1)
    fresh_index = lax.broadcasted_iota(jnp.int32, (16, 16), 1)
    step = lax.broadcasted_iota(jnp.int32, (16, 16), 0) & 1
    by_rows = (((1,), (1,)), ((), ()))
    first_row = (own_ref[0] >> 3) * ROWS
    place = own_ref[0] & (TP - 1)
    for k in range(TP):
        qkv[pl.ds((place ^ k) * 2, 2)] = blocks[k][...]
    load.wait()
    place_pages(plan_ref, received_ref, moved_ref)
    store.start()

    @pl.loop(0, ROWS, step=4)
    def _(base):
        for i in range(4):
            r = base + i
            queries = qkv[r, 0:16, :]
            length = lengths_ref[first_row + r]
            for j in range(MAXP):
                page = moved_ref[table_ref[j, r]]
                part = lax.dot_general(queries, page, by_rows, preferred_element_type=jnp.float32)
                part = jnp.where(position + j * PAGE < length, part * scale, -jnp.inf)
                scores[r, :, j * PAGE : (j + 1) * PAGE] = part
            part = lax.dot_general(
                queries, qkv[r, 16:32, :], by_rows, preferred_element_type=jnp.float32
            )
            fresh_scores[r] = jnp.where(fresh_index <= step, part * scale, -jnp.inf)

    @pl.loop(0, ROWS, step=4)
    def _(base):
        rows = pl.ds(base, 4)
        cache, fresh = scores[rows], fresh_scores[rows]
        top = jnp.maximum(
            jnp.max(cache, axis=-1, keepdims=True), jnp.max(fresh, axis=-1, keepdims=True)
        )
        cache, fresh = jnp.exp(cache - top), jnp.exp(fresh - top)
        total = jnp.sum(cache, axis=-1, keepdims=True) + jnp.sum(fresh, axis=-1, keepdims=True)
        cache_ref[rows] = (cache / total).astype(jnp.bfloat16)
        fresh = (fresh / total).astype(jnp.bfloat16).astype(jnp.float32)
        values = qkv[rows, 32:48, :].astype(jnp.float32)
        known_ref[rows] = fresh[:, :, 0:1] * values[:, 0:1, :] + fresh[:, :, 1:2] * values[:, 1:2, :]

    @pl.loop(0, ROWS)
    def _(r):
        @pl.when(plan_ref[6, r] < 0)
        def _():
            cached = jnp.zeros((16, HD), jnp.float32)
            for j in range(MAXP):
                weights = cache_ref[r, :, j * PAGE : (j + 1) * PAGE]
                page = values_ref[table_ref[j, r]]
                cached += jnp.dot(weights, page, preferred_element_type=jnp.float32)
            known_ref[r] += cached

    store.wait()


def keys_step(own, plan, table, lengths, pool, received, values, blocks):
    return pl.pallas_call(
        keys_kernel,
        out_shape=(
            jax.ShapeDtypeStruct((POOL, PAGE, HD), jnp.bfloat16),
            jax.ShapeDtypeStruct((ROWS, 16, MAXP * PAGE), jnp.bfloat16),
            jax.ShapeDtypeStruct((ROWS, 16, HD), jnp.float32),
        ),
        in_specs=[spec(SMEM)] * 4 + [spec(pl.ANY)] + [spec(VMEM)] * (2 + TP),
        out_specs=(spec(pl.ANY), spec(VMEM), spec(VMEM)),
        scratch_shapes=[
            pltpu.VMEM((POOL, PAGE, HD), jnp.bfloat16),
            pltpu.SemaphoreType.DMA((2,)),
            pltpu.VMEM((ROWS, QKV, HD), jnp.bfloat16),
            pltpu.VMEM((ROWS, 16, MAXP * PAGE), jnp.float32),
            pltpu.VMEM((ROWS, 16, 16), jnp.float32),
        ],
        compiler_params=LIMIT,
        cost_estimate=cost(8_000_000),
    )(own, plan, table, lengths, pool, received, values, *blocks)


def values_kernel(plan_ref, cache_ref, known_ref, received_ref, out_ref, mixed):
    mixed[...] = known_ref[...]
    for k in range(MOVES):
        r = plan_ref[5, k * MAXP]
        values = received_ref[:, k].reshape(MAXP * PAGE, HD)
        mixed[r] = known_ref[r] + jnp.dot(
            cache_ref[r], values, preferred_element_type=jnp.float32
        )
    for r in range(ROWS):
        row = mixed[r]
        for g in range(GROUP):
            head = row[2 * g : 2 * g + 2, :].astype(jnp.bfloat16)
            out_ref[r, :, g * HD : (g + 1) * HD] = head


def values_step(plan, weights, known, received):
    return pl.pallas_call(
        values_kernel,
        out_shape=jax.ShapeDtypeStruct((ROWS, 2, GROUP * HD), jnp.bfloat16),
        in_specs=[spec(SMEM)] + [spec(VMEM)] * 3,
        out_specs=spec(VMEM),
        scratch_shapes=[pltpu.VMEM((ROWS, 16, HD), jnp.float32)],
        compiler_params=LIMIT,
        cost_estimate=cost(4_000_000),
    )(plan, weights, known, received)


def place_kernel(plan_ref, pool_ref, received_ref, out_ref):
    out_ref[...] = pool_ref[...]
    place_pages(plan_ref, received_ref, out_ref)


def place_step(plan, pool, received):
    return pl.pallas_call(
        place_kernel,
        out_shape=jax.ShapeDtypeStruct((POOL, PAGE, HD), jnp.bfloat16),
        in_specs=[spec(SMEM)] + [spec(VMEM)] * 2,
        out_specs=spec(VMEM),
        compiler_params=LIMIT,
        cost_estimate=cost(8_000_000),
    )(plan, pool, received)


def swap(array, axes):
    return lax.all_to_all(array, axes, split_axis=0, concat_axis=0, tiled=True)


def cross(array):
    return lax.ppermute(array, "zh", [(0, 1), (1, 0)])


def move_and_attend(
    slots, cap, own, plan, table, lengths, new_queries, new_keys, new_values, key_pool, value_pool
):
    direct, send = outgoing(plan, key_pool, value_pool, slots)
    direct = cross(direct)
    held = swap(send, ("y", "x")).reshape(SPREAD * slots, 2, PR, HD)
    direct, leaving_keys, leaving_values = crossing(plan, held, cap, direct, *touch(direct))
    later_keys = cross(leaving_keys)
    leaving_values, token = touch(later_keys, leaving_values)
    later_values = cross(leaving_values)
    direct = swap(direct, ("y", "x")).reshape(SPREAD * WHOLE, 2, PR, HD)
    final_keys = deliver(plan, held, direct, later_keys, 0, 4_000_000, token)
    received_keys = swap(final_keys.reshape(SPREAD, MOVES, PR, HD), ("y", "x"))
    final_values, token = deliver(plan, held, direct, later_values, 1, FILLER)
    blocks = list(pack(own, new_queries, new_keys, new_values, token))
    for k in range(1, TP):
        blocks[k] = lax.ppermute(blocks[k], ("zl", "c"), [(i, i ^ k) for i in range(TP)])
    received_values = swap(final_values.reshape(SPREAD, MOVES, PR, HD), ("y", "x"))
    key_moved, weights, known = keys_step(
        own, plan, table, lengths, key_pool, received_keys, value_pool, blocks
    )
    return key_moved, weights, known, received_values


def body(
    new_queries,
    new_keys,
    new_values,
    key_pool,
    value_pool,
    lengths,
    page_table,
    mig_row,
    mig_source,
    mig_pages,
):
    own = lax.axis_index(("y", "zh", "x", "zl", "c")).astype(jnp.int32).reshape(1)
    plan, branch = make_plan(own, mig_row, mig_source, mig_pages, page_table)
    key_moved, weights, known, received_values = lax.switch(
        branch[0],
        [functools.partial(move_and_attend, slots, cap) for slots, cap in BRANCHES],
        own,
        plan,
        page_table.T,
        lengths,
        new_queries,
        new_keys,
        new_values,
        key_pool,
        value_pool,
    )
    mixed = values_step(plan, weights, known, received_values)
    attention = lax.all_to_all(mixed, ("zl", "c"), split_axis=0, concat_axis=2, tiled=True)
    value_moved = place_step(plan, value_pool, received_values)
    return (attention, key_moved, value_moved)


def solution(mesh):
    fine = Mesh(mesh.devices.reshape(4, NZ, NX, 4, 2), ("y", "zh", "x", "zl", "c"))
    inst, tp = ("y", "zh", "x"), ("zl", "c")
    rows = P(inst + tp, None, None)
    pool = P(inst, None, tp)
    return jax.shard_map(
        body,
        mesh=fine,
        in_specs=(rows, rows, rows, pool, pool, P(), P(inst, None), P(), P(), P()),
        out_specs=(rows, pool, pool),
        check_vma=False,
    )
```

```python
import functools
import math

import jax
import jax.numpy as jnp
from jax import lax
from jax.experimental import pallas as pl
from jax.experimental.pallas import tpu as pltpu
from jax.sharding import Mesh
from jax.sharding import PartitionSpec as P

HD = 128
PAGE = 128
MAXP = 4
ROWS = 16
POOL = 64
MOVES = 11
MIGS = 352
NX = 4
NZ = 2
TP = 8
GROUP = 8
SPREAD = 16
PIECES = SPREAD * MOVES
WIDTH = 256
WHOLE = 3
BRANCHES = ((MOVES, SPREAD * (MOVES - WHOLE)), (MOVES - 2, 52), (MOVES - 3, 48))
PR = PAGE * MAXP // SPREAD
QKV = 48
VMEM = pltpu.VMEM
SMEM = pltpu.SMEM
HBM = pltpu.HBM
FILLER = 100_000_000_000
LIMIT = pltpu.CompilerParams(vmem_limit_bytes=40 * 1024 * 1024)
ROOM = pltpu.CompilerParams(vmem_limit_bytes=62_300_000)
ALONE = pltpu.CompilerParams(vmem_limit_bytes=63_400_000)


def spec(space):
    return pl.BlockSpec(memory_space=space)


def cost(bytes_accessed):
    return pl.CostEstimate(flops=100 * bytes_accessed, bytes_accessed=bytes_accessed, transcendentals=0)


def place_of(inst):
    half = (inst >> 2) & 1
    place = ((inst >> 3) << 2) | (inst & 3)
    return half, place


def plan_kernel(own_ref, row_ref, src_ref, pages_ref, table_ref, out_ref, branch_ref):
    own = own_ref[0] >> 3
    half, _ = place_of(own)
    sub = lax.broadcasted_iota(jnp.int32, (MIGS, MIGS), 0)
    lane = lax.broadcasted_iota(jnp.int32, (MIGS, MIGS), 1)

    def to_column(row):
        spread = jnp.where(sub == lane, row.astype(jnp.float32), 0.0)
        return jnp.sum(spread, axis=1, keepdims=True).astype(jnp.int32)

    def to_row(column):
        spread = jnp.where(sub == lane, column.astype(jnp.float32), 0.0)
        return jnp.sum(spread, axis=0, keepdims=True).astype(jnp.int32)

    def count(same):
        return jnp.sum(jnp.where(same, 1.0, 0.0), axis=1, keepdims=True).astype(jnp.int32)

    row_r = row_ref[...].reshape(1, MIGS)
    src_r = src_ref[...].reshape(1, MIGS)
    row_c, src_c = to_column(row_r), to_column(src_r)
    tgt_r, tgt_c = row_r >> 4, row_c >> 4
    sh_r, _ = place_of(src_r)
    th_r, _ = place_of(tgt_r)
    sh_c, sp_c = place_of(src_c)
    th_c, tp_c = place_of(tgt_c)
    before = lane < sub
    same_src = src_c == src_r
    crosses = sh_r != th_r
    rank_src = count(before & same_src)
    rank_tgt = count(before & (tgt_c == tgt_r))
    rank_out = count(before & same_src & crosses)
    fewest = jnp.min(count(same_src & crosses), axis=0, keepdims=True)
    crosses_c = sh_c != th_c
    direct = crosses_c & (rank_out < WHOLE)
    later = crosses_c & (rank_out >= WHOLE)
    needed = jnp.zeros((1, 1), jnp.float32)
    for side in range(NZ):
        leaving = jnp.where(later & (sh_c == side), 1.0, 0.0)
        needed = jnp.maximum(needed, jnp.sum(leaving, axis=0, keepdims=True))
    needed = needed.astype(jnp.int32)
    branch = jnp.zeros((1, 1), jnp.int32)
    slots = jnp.full((1, 1), BRANCHES[0][0], jnp.int32)
    for index, (slots_i, cap) in enumerate(BRANCHES):
        fits = (jnp.minimum(fewest, WHOLE) >= MOVES - slots_i) & (needed <= cap)
        branch = jnp.where(fits, index, branch)
        slots = jnp.where(fits, slots_i, slots)
    rank_rest = rank_src - jnp.minimum(rank_out, WHOLE)
    later_r = to_row(jnp.where(later, 1, 0)) > 0
    rank_later = count(before & later_r & (sh_c == sh_r))
    rest_place = sp_c * slots + rank_rest
    direct_place = SPREAD * slots + sp_c * WHOLE + rank_out
    origin = jnp.where(sh_c == th_c, rest_place, SPREAD * (slots + WHOLE) + rank_later)
    origin = jnp.where(direct, direct_place, origin)
    final_place = tp_c * MOVES + rank_tgt
    col = lax.broadcasted_iota(jnp.int32, (1, WIDTH), 1)
    message, page = col >> 2, col & 3

    def pick(chosen, value):
        picked = jnp.where(chosen, value.astype(jnp.float32), 0.0)
        return jnp.sum(picked, axis=0, keepdims=True).astype(jnp.int32)

    def by_page(pages):
        chosen = pages[MAXP - 1]
        for j in range(MAXP - 1):
            chosen = jnp.where(page == j, pages[j], chosen)
        return chosen

    out_ref[0:1, :] = pick(later & (sh_c == half) & (rank_later == col), rest_place)
    out_ref[1:2, :] = pick((th_c == half) & (final_place == col), origin)
    pages = by_page([to_column(pages_ref[j : j + 1, :]) for j in range(MAXP)])
    mine = src_c == own
    out_ref[2:3, :] = pick(mine & ~direct & (rank_rest == message), pages)
    arrival = pick((tgt_c == own) & (rank_tgt == message), row_c & (ROWS - 1))
    sub16 = lax.broadcasted_iota(jnp.int32, (ROWS, ROWS), 0)
    lane16 = lax.broadcasted_iota(jnp.int32, (ROWS, ROWS), 1)

    def table_column(j):
        spread = jnp.where(sub16 == lane16, table_ref[j : j + 1, :].astype(jnp.float32), 0.0)
        return jnp.sum(spread, axis=1, keepdims=True).astype(jnp.int32)

    table = by_page([table_column(j) for j in range(MAXP)])
    row_id = lax.broadcasted_iota(jnp.int32, (ROWS, WIDTH), 0)
    out_ref[3:4, :] = pick(row_id == arrival, table)
    out_ref[4:5, :] = pick(mine & direct & (rank_out == message), pages)
    out_ref[5:6, :] = arrival
    branch_ref[0] = branch[0, 0]
    out_ref[6:7, :] = pick((tgt_c == own) & ((row_c & (ROWS - 1)) == col), rank_tgt + 1) - 1
    out_ref[7:8, :] = jnp.zeros((1, WIDTH), jnp.int32)


def make_plan(own, mig_row, mig_source, mig_pages, page_table):
    return pl.pallas_call(
        plan_kernel,
        out_shape=(
            jax.ShapeDtypeStruct((8, WIDTH), jnp.int32),
            jax.ShapeDtypeStruct((1,), jnp.int32),
        ),
        in_specs=[spec(SMEM), spec(VMEM), spec(VMEM), spec(VMEM), spec(VMEM)],
        out_specs=(spec(VMEM), spec(SMEM)),
        compiler_params=ALONE,
        cost_estimate=cost(100_000),
    )(own, mig_row, mig_source, mig_pages.T, page_table.T)


def pack_kernel(own_ref, q_ref, k_ref, v_ref, after_ref, *refs):
    blocks, scratch = refs[:TP], refs[TP]
    scratch[...] = jnp.zeros_like(scratch)
    place = own_ref[0] & (TP - 1)

    @pl.loop(0, TP)
    def _(k):
        d = place ^ k
        own_head = pl.ds(pl.multiple_of(d * HD, HD), HD)
        for r in range(2):
            for g in range(GROUP):
                head = pl.ds(pl.multiple_of((d * GROUP + g) * HD, HD), HD)
                scratch[k, r, 2 * g : 2 * g + 2, :] = q_ref[r, :, head].astype(jnp.float32)
            scratch[k, r, 16:18, :] = k_ref[r, :, own_head].astype(jnp.float32)
            scratch[k, r, 32:34, :] = v_ref[r, :, own_head].astype(jnp.float32)

    for k in range(TP):
        blocks[k][...] = scratch[k].astype(jnp.bfloat16)


def pack(own, new_queries, new_keys, new_values, after):
    return pl.pallas_call(
        pack_kernel,
        out_shape=(jax.ShapeDtypeStruct((2, QKV, HD), jnp.bfloat16),) * TP,
        in_specs=[spec(SMEM)] + [spec(VMEM)] * 3 + [spec(pl.ANY)],
        out_specs=(spec(VMEM),) * TP,
        scratch_shapes=[pltpu.VMEM((TP, 2, QKV, HD), jnp.float32)],
        compiler_params=LIMIT,
        cost_estimate=cost(400_000),
    )(own, new_queries, new_keys, new_values, after)


def load_pages(plan_ref, row, messages, pools, target, j, sem):
    for m in range(messages):
        for part, pool in enumerate(pools):
            source = pool.at[plan_ref[row, m * MAXP + j]]
            slot = target.at[pl.ds(MAXP * j, MAXP), m, part]
            pltpu.make_async_copy(source, slot, sem).start()


def wait_for(target, sem):
    pltpu.make_async_copy(target, target, sem).wait()


def send_whole_kernel(plan_ref, keys_ref, values_ref, out_ref, sem):
    for j in range(MAXP):
        load_pages(plan_ref, 4, WHOLE, (keys_ref, values_ref), out_ref, j, sem.at[0])
    wait_for(out_ref, sem.at[0])


def send_rest_kernel(slots, plan_ref, keys_ref, values_ref, after_ref, out_ref, held, in_sem, out_sem):
    for j in range(MAXP):
        load_pages(plan_ref, 2, slots, (keys_ref, values_ref), held, j, in_sem.at[j])
    sends = []
    for j in range(MAXP):
        block = pl.ds(MAXP * j, MAXP)
        wait_for(held.at[block], in_sem.at[j])
        send = pltpu.make_async_copy(held.at[block], out_ref.at[block], out_sem.at[j])
        send.start()
        sends.append(send)
    for send in sends:
        send.wait()


def send_whole(plan, keys, values):
    return pl.pallas_call(
        send_whole_kernel,
        out_shape=jax.ShapeDtypeStruct((SPREAD, WHOLE, 2, PR, HD), jnp.bfloat16),
        in_specs=[spec(SMEM)] + [spec(pl.ANY)] * 2,
        out_specs=spec(VMEM),
        scratch_shapes=[pltpu.SemaphoreType.DMA((1,))],
        compiler_params=ROOM,
        cost_estimate=cost(2_000_000),
    )(plan, keys, values)


def send_rest(plan, keys, values, slots, after):
    held = (SPREAD, slots, 2, PR, HD)
    return pl.pallas_call(
        functools.partial(send_rest_kernel, slots),
        out_shape=jax.ShapeDtypeStruct(held, jnp.bfloat16),
        in_specs=[spec(SMEM)] + [spec(pl.ANY)] * 3,
        out_specs=spec(HBM),
        scratch_shapes=[
            pltpu.VMEM(held, jnp.bfloat16),
            pltpu.SemaphoreType.DMA((MAXP,)),
            pltpu.SemaphoreType.DMA((MAXP,)),
        ],
        compiler_params=ROOM,
        cost_estimate=cost(FILLER),
    )(plan, keys, values, after)


def touch_kernel(*refs):
    refs[-1][...] = jnp.zeros_like(refs[-1])


def touch(array, *through):
    kept = [jax.ShapeDtypeStruct(a.shape, a.dtype) for a in through]
    return pl.pallas_call(
        touch_kernel,
        out_shape=tuple(kept) + (jax.ShapeDtypeStruct((8, HD), jnp.float32),),
        in_specs=[spec(pl.ANY)] * (1 + len(kept)),
        out_specs=(spec(pl.ANY),) * len(kept) + (spec(VMEM),),
        input_output_aliases={1 + i: i for i in range(len(kept))},
        cost_estimate=cost(FILLER),
    )(array, *through)


def cross_kernel(cap, plan_ref, held_ref, *refs):
    keys_ref, values_ref = refs[-2:]

    @pl.loop(0, cap, step=4)
    def _(base):
        for i in range(4):
            place = plan_ref[0, base + i]
            keys_ref[base + i] = held_ref[place, 0]
            values_ref[base + i] = held_ref[place, 1]


def crossing(plan, held, cap, through, after):
    piece = jax.ShapeDtypeStruct((cap, PR, HD), jnp.bfloat16)
    return pl.pallas_call(
        functools.partial(cross_kernel, cap),
        out_shape=(jax.ShapeDtypeStruct(through.shape, through.dtype), piece, piece),
        in_specs=[spec(SMEM), spec(VMEM), spec(pl.ANY), spec(pl.ANY)],
        out_specs=(spec(pl.ANY), spec(VMEM), spec(VMEM)),
        input_output_aliases={2: 0},
        compiler_params=ALONE,
        cost_estimate=cost(4_000_000),
    )(plan, held, through, after)


def deliver_kernel(slots, part, unread, plan_ref, rest_ref, direct_ref, later_ref, *refs):
    gathered, ordered, in_sem, out_sem = refs[-4:]
    out_ref = refs[unread]
    if part:
        refs[unread + 1][...] = jnp.zeros_like(refs[unread + 1])
    kept = SPREAD * slots
    crossed = kept + SPREAD * WHOLE
    moves = [
        (rest_ref.at[:, part], gathered.at[0:kept]),
        (direct_ref.at[:, part], gathered.at[kept:crossed]),
        (later_ref, gathered.at[crossed:]),
    ]
    copies = [pltpu.make_async_copy(a, b, in_sem.at[i]) for i, (a, b) in enumerate(moves)]
    for copy in copies:
        copy.start()
    for copy in copies:
        copy.wait()
    step = PIECES // 4
    sends = []
    for quarter in range(4):
        first = quarter * step

        @pl.loop(first, first + step, step=11)
        def _(base):
            for i in range(11):
                ordered[base + i] = gathered[plan_ref[1, base + i]]

        block = pl.ds(first, step)
        send = pltpu.make_async_copy(ordered.at[block], out_ref.at[block], out_sem.at[quarter])
        send.start()
        sends.append(send)
    for send in sends:
        send.wait()


def deliver(plan, rest, direct, later, part, beside, *after):
    slots, cap = rest.shape[0] // SPREAD, later.shape[0]
    shapes = (
        jax.ShapeDtypeStruct((PIECES, PR, HD), jnp.bfloat16),
        jax.ShapeDtypeStruct((8, HD), jnp.float32),
    )
    return pl.pallas_call(
        functools.partial(deliver_kernel, slots, part, len(after)),
        out_shape=shapes if part else shapes[0],
        in_specs=[spec(SMEM)] + [spec(pl.ANY)] * (3 + len(after)),
        out_specs=(spec(HBM), spec(VMEM)) if part else spec(HBM),
        scratch_shapes=[
            pltpu.VMEM((SPREAD * (slots + WHOLE) + cap, PR, HD), jnp.bfloat16),
            pltpu.VMEM((PIECES, PR, HD), jnp.bfloat16),
            pltpu.SemaphoreType.DMA((3,)),
            pltpu.SemaphoreType.DMA((4,)),
        ],
        compiler_params=ALONE,
        cost_estimate=cost(beside),
    )(plan, rest, direct, later, *after)


def place_pages(plan_ref, received_ref, moved):
    @pl.loop(0, MOVES)
    def _(k):
        for j in range(MAXP):
            page = plan_ref[3, k * MAXP + j]
            for quarter in range(MAXP):
                first = quarter * PR
                moved[page, first : first + PR, :] = received_ref[MAXP * j + quarter, k]


def keys_kernel(own_ref, plan_ref, table_ref, lengths_ref, pool_ref, received_ref, values_ref, *refs):
    blocks, (out_ref, cache_ref, known_ref, moved_ref, sem, qkv, scores, fresh_scores) = refs[:TP], refs[TP:]
    load = pltpu.make_async_copy(pool_ref, moved_ref, sem.at[0])
    store = pltpu.make_async_copy(moved_ref, out_ref, sem.at[1])
    load.start()
    scale = 1.0 / math.sqrt(HD)
    position = lax.broadcasted_iota(jnp.int32, (16, PAGE), 1)
    fresh_index = lax.broadcasted_iota(jnp.int32, (16, 16), 1)
    step = lax.broadcasted_iota(jnp.int32, (16, 16), 0) & 1
    by_rows = (((1,), (1,)), ((), ()))
    first_row = (own_ref[0] >> 3) * ROWS
    place = own_ref[0] & (TP - 1)
    for k in range(TP):
        qkv[pl.ds((place ^ k) * 2, 2)] = blocks[k][...]
    load.wait()
    place_pages(plan_ref, received_ref, moved_ref)
    store.start()

    @pl.loop(0, ROWS, step=4)
    def _(base):
        for i in range(4):
            r = base + i
            queries = qkv[r, 0:16, :]
            length = lengths_ref[first_row + r]
            for j in range(MAXP):
                page = moved_ref[table_ref[j, r]]
                part = lax.dot_general(queries, page, by_rows, preferred_element_type=jnp.float32)
                part = jnp.where(position + j * PAGE < length, part * scale, -jnp.inf)
                scores[r, :, j * PAGE : (j + 1) * PAGE] = part
            part = lax.dot_general(
                queries, qkv[r, 16:32, :], by_rows, preferred_element_type=jnp.float32
            )
            fresh_scores[r] = jnp.where(fresh_index <= step, part * scale, -jnp.inf)

    @pl.loop(0, ROWS, step=4)
    def _(base):
        rows = pl.ds(base, 4)
        cache, fresh = scores[rows], fresh_scores[rows]
        top = jnp.maximum(
            jnp.max(cache, axis=-1, keepdims=True), jnp.max(fresh, axis=-1, keepdims=True)
        )
        cache, fresh = jnp.exp(cache - top), jnp.exp(fresh - top)
        total = jnp.sum(cache, axis=-1, keepdims=True) + jnp.sum(fresh, axis=-1, keepdims=True)
        cache_ref[rows] = (cache / total).astype(jnp.bfloat16)
        fresh = (fresh / total).astype(jnp.bfloat16).astype(jnp.float32)
        values = qkv[rows, 32:48, :].astype(jnp.float32)
        known_ref[rows] = fresh[:, :, 0:1] * values[:, 0:1, :] + fresh[:, :, 1:2] * values[:, 1:2, :]

    @pl.loop(0, ROWS)
    def _(r):
        @pl.when(plan_ref[6, r] < 0)
        def _():
            cached = jnp.zeros((16, HD), jnp.float32)
            for j in range(MAXP):
                weights = cache_ref[r, :, j * PAGE : (j + 1) * PAGE]
                page = values_ref[table_ref[j, r]]
                cached += jnp.dot(weights, page, preferred_element_type=jnp.float32)
            known_ref[r] += cached

    store.wait()


def keys_step(own, plan, table, lengths, pool, received, values, blocks):
    return pl.pallas_call(
        keys_kernel,
        out_shape=(
            jax.ShapeDtypeStruct((POOL, PAGE, HD), jnp.bfloat16),
            jax.ShapeDtypeStruct((ROWS, 16, MAXP * PAGE), jnp.bfloat16),
            jax.ShapeDtypeStruct((ROWS, 16, HD), jnp.float32),
        ),
        in_specs=[spec(SMEM)] * 4 + [spec(pl.ANY)] + [spec(VMEM)] * (2 + TP),
        out_specs=(spec(pl.ANY), spec(VMEM), spec(VMEM)),
        scratch_shapes=[
            pltpu.VMEM((POOL, PAGE, HD), jnp.bfloat16),
            pltpu.SemaphoreType.DMA((2,)),
            pltpu.VMEM((ROWS, QKV, HD), jnp.bfloat16),
            pltpu.VMEM((ROWS, 16, MAXP * PAGE), jnp.float32),
            pltpu.VMEM((ROWS, 16, 16), jnp.float32),
        ],
        compiler_params=LIMIT,
        cost_estimate=cost(8_000_000),
    )(own, plan, table, lengths, pool, received, values, *blocks)


def values_kernel(plan_ref, cache_ref, known_ref, received_ref, out_ref, mixed):
    mixed[...] = known_ref[...]
    for k in range(MOVES):
        r = plan_ref[5, k * MAXP]
        values = received_ref[:, k].reshape(MAXP * PAGE, HD)
        mixed[r] = known_ref[r] + jnp.dot(
            cache_ref[r], values, preferred_element_type=jnp.float32
        )
    for r in range(ROWS):
        row = mixed[r]
        for g in range(GROUP):
            head = row[2 * g : 2 * g + 2, :].astype(jnp.bfloat16)
            out_ref[r, :, g * HD : (g + 1) * HD] = head


def values_step(plan, weights, known, received):
    return pl.pallas_call(
        values_kernel,
        out_shape=jax.ShapeDtypeStruct((ROWS, 2, GROUP * HD), jnp.bfloat16),
        in_specs=[spec(SMEM)] + [spec(VMEM)] * 3,
        out_specs=spec(VMEM),
        scratch_shapes=[pltpu.VMEM((ROWS, 16, HD), jnp.float32)],
        compiler_params=LIMIT,
        cost_estimate=cost(4_000_000),
    )(plan, weights, known, received)


def place_kernel(plan_ref, pool_ref, received_ref, out_ref, moved, arrived, sem):
    pairs = [(pool_ref, moved), (received_ref, arrived)]
    loads = [pltpu.make_async_copy(a, b, sem.at[i]) for i, (a, b) in enumerate(pairs)]
    store = pltpu.make_async_copy(moved, out_ref, sem.at[2])
    for load in loads:
        load.start()
    for load in loads:
        load.wait()
    place_pages(plan_ref, arrived, moved)
    store.start()
    store.wait()


def place_step(plan, pool, received):
    return pl.pallas_call(
        place_kernel,
        out_shape=jax.ShapeDtypeStruct((POOL, PAGE, HD), jnp.bfloat16),
        in_specs=[spec(SMEM), spec(pl.ANY), spec(pl.ANY)],
        out_specs=spec(pl.ANY),
        scratch_shapes=[
            pltpu.VMEM((POOL, PAGE, HD), jnp.bfloat16),
            pltpu.VMEM((SPREAD, MOVES, PR, HD), jnp.bfloat16),
            pltpu.SemaphoreType.DMA((3,)),
        ],
        compiler_params=LIMIT,
        cost_estimate=cost(8_000_000),
    )(plan, pool, received)


def swap(array, axes):
    return lax.all_to_all(array, axes, split_axis=0, concat_axis=0, tiled=True)


def cross(array):
    return lax.ppermute(array, "zh", [(0, 1), (1, 0)])


def move_and_attend(
    slots, cap, own, plan, table, lengths, new_queries, new_keys, new_values, key_pool, value_pool
):
    pages = [pool.reshape(POOL, MAXP, PR, HD) for pool in (key_pool, value_pool)]
    direct = send_whole(plan, *pages)
    send = send_rest(plan, *pages, slots, direct)
    direct = cross(direct)
    held = swap(send, ("y", "x")).reshape(SPREAD * slots, 2, PR, HD)
    direct, leaving_keys, leaving_values = crossing(plan, held, cap, direct, *touch(direct))
    later_keys = cross(leaving_keys)
    leaving_values, token = touch(later_keys, leaving_values)
    later_values = cross(leaving_values)
    direct = swap(direct, ("y", "x")).reshape(SPREAD * WHOLE, 2, PR, HD)
    final_keys = deliver(plan, held, direct, later_keys, 0, 4_000_000, token)
    received_keys = swap(final_keys.reshape(SPREAD, MOVES, PR, HD), ("y", "x"))
    final_values, token = deliver(plan, held, direct, later_values, 1, FILLER)
    blocks = list(pack(own, new_queries, new_keys, new_values, token))
    for k in range(1, TP):
        blocks[k] = lax.ppermute(blocks[k], ("zl", "c"), [(i, i ^ k) for i in range(TP)])
    received_values = swap(final_values.reshape(SPREAD, MOVES, PR, HD), ("y", "x"))
    key_moved, weights, known = keys_step(
        own, plan, table, lengths, key_pool, received_keys, value_pool, blocks
    )
    return key_moved, weights, known, received_values


def body(
    new_queries,
    new_keys,
    new_values,
    key_pool,
    value_pool,
    lengths,
    page_table,
    mig_row,
    mig_source,
    mig_pages,
):
    own = lax.axis_index(("y", "zh", "x", "zl", "c")).astype(jnp.int32).reshape(1)
    plan, branch = make_plan(own, mig_row, mig_source, mig_pages, page_table)
    key_moved, weights, known, received_values = lax.switch(
        branch[0],
        [functools.partial(move_and_attend, slots, cap) for slots, cap in BRANCHES],
        own,
        plan,
        page_table.T,
        lengths,
        new_queries,
        new_keys,
        new_values,
        key_pool,
        value_pool,
    )
    mixed = values_step(plan, weights, known, received_values)
    attention = lax.all_to_all(mixed, ("zl", "c"), split_axis=0, concat_axis=2, tiled=True)
    value_moved = place_step(plan, value_pool, received_values)
    return (attention, key_moved, value_moved)


def solution(mesh):
    fine = Mesh(mesh.devices.reshape(4, NZ, NX, 4, 2), ("y", "zh", "x", "zl", "c"))
    inst, tp = ("y", "zh", "x"), ("zl", "c")
    rows = P(inst + tp, None, None)
    pool = P(inst, None, tp)
    return jax.shard_map(
        body,
        mesh=fine,
        in_specs=(rows, rows, rows, pool, pool, P(), P(inst, None), P(), P(), P()),
        out_specs=(rows, pool, pool),
        check_vma=False,
    )
```

```python
import functools
import math

import jax
import jax.numpy as jnp
from jax import lax
from jax.experimental import pallas as pl
from jax.experimental.pallas import tpu as pltpu
from jax.sharding import Mesh
from jax.sharding import PartitionSpec as P

HD = 128
PAGE = 128
MAXP = 4
ROWS = 16
POOL = 64
MOVES = 11
MIGS = 352
NX = 4
NZ = 2
TP = 8
GROUP = 8
SPREAD = 16
PIECES = SPREAD * MOVES
WIDTH = 256
WHOLE = 3
BRANCHES = ((MOVES, SPREAD * (MOVES - WHOLE)), (MOVES - 2, 52), (MOVES - 3, 48))
PR = PAGE * MAXP // SPREAD
QKV = 32
VMEM = pltpu.VMEM
SMEM = pltpu.SMEM
HBM = pltpu.HBM
FILLER = 100_000_000_000
LIMIT = pltpu.CompilerParams(vmem_limit_bytes=40 * 1024 * 1024)
ROOM = pltpu.CompilerParams(vmem_limit_bytes=62_300_000)
ALONE = pltpu.CompilerParams(vmem_limit_bytes=63_400_000)


def spec(space):
    return pl.BlockSpec(memory_space=space)


def cost(bytes_accessed):
    return pl.CostEstimate(flops=100 * bytes_accessed, bytes_accessed=bytes_accessed, transcendentals=0)


def place_of(inst):
    half = (inst >> 2) & 1
    place = ((inst >> 3) << 2) | (inst & 3)
    return half, place


def plan_kernel(own_ref, row_ref, src_ref, pages_ref, table_ref, out_ref, branch_ref):
    own = own_ref[0] >> 3
    half, _ = place_of(own)
    sub = lax.broadcasted_iota(jnp.int32, (MIGS, MIGS), 0)
    lane = lax.broadcasted_iota(jnp.int32, (MIGS, MIGS), 1)

    def to_column(row):
        spread = jnp.where(sub == lane, row.astype(jnp.float32), 0.0)
        return jnp.sum(spread, axis=1, keepdims=True).astype(jnp.int32)

    def to_row(column):
        spread = jnp.where(sub == lane, column.astype(jnp.float32), 0.0)
        return jnp.sum(spread, axis=0, keepdims=True).astype(jnp.int32)

    def count(same):
        return jnp.sum(jnp.where(same, 1.0, 0.0), axis=1, keepdims=True).astype(jnp.int32)

    row_r = row_ref[...].reshape(1, MIGS)
    src_r = src_ref[...].reshape(1, MIGS)
    row_c, src_c = to_column(row_r), to_column(src_r)
    tgt_r, tgt_c = row_r >> 4, row_c >> 4
    sh_r, _ = place_of(src_r)
    th_r, _ = place_of(tgt_r)
    sh_c, sp_c = place_of(src_c)
    th_c, tp_c = place_of(tgt_c)
    before = lane < sub
    same_src = src_c == src_r
    crosses = sh_r != th_r
    rank_src = count(before & same_src)
    rank_tgt = count(before & (tgt_c == tgt_r))
    rank_out = count(before & same_src & crosses)
    fewest = jnp.min(count(same_src & crosses), axis=0, keepdims=True)
    crosses_c = sh_c != th_c
    direct = crosses_c & (rank_out < WHOLE)
    later = crosses_c & (rank_out >= WHOLE)
    needed = jnp.zeros((1, 1), jnp.float32)
    for side in range(NZ):
        leaving = jnp.where(later & (sh_c == side), 1.0, 0.0)
        needed = jnp.maximum(needed, jnp.sum(leaving, axis=0, keepdims=True))
    needed = needed.astype(jnp.int32)
    branch = jnp.zeros((1, 1), jnp.int32)
    slots = jnp.full((1, 1), BRANCHES[0][0], jnp.int32)
    for index, (slots_i, cap) in enumerate(BRANCHES):
        fits = (jnp.minimum(fewest, WHOLE) >= MOVES - slots_i) & (needed <= cap)
        branch = jnp.where(fits, index, branch)
        slots = jnp.where(fits, slots_i, slots)
    rank_rest = rank_src - jnp.minimum(rank_out, WHOLE)
    later_r = to_row(jnp.where(later, 1, 0)) > 0
    rank_later = count(before & later_r & (sh_c == sh_r))
    rest_place = sp_c * slots + rank_rest
    direct_place = SPREAD * slots + sp_c * WHOLE + rank_out
    origin = jnp.where(sh_c == th_c, rest_place, SPREAD * (slots + WHOLE) + rank_later)
    origin = jnp.where(direct, direct_place, origin)
    final_place = tp_c * MOVES + rank_tgt
    col = lax.broadcasted_iota(jnp.int32, (1, WIDTH), 1)
    message, page = col >> 2, col & 3

    def pick(chosen, value):
        picked = jnp.where(chosen, value.astype(jnp.float32), 0.0)
        return jnp.sum(picked, axis=0, keepdims=True).astype(jnp.int32)

    def by_page(pages):
        chosen = pages[MAXP - 1]
        for j in range(MAXP - 1):
            chosen = jnp.where(page == j, pages[j], chosen)
        return chosen

    out_ref[0:1, :] = pick(later & (sh_c == half) & (rank_later == col), rest_place)
    out_ref[1:2, :] = pick((th_c == half) & (final_place == col), origin)
    pages = by_page([to_column(pages_ref[j : j + 1, :]) for j in range(MAXP)])
    mine = src_c == own
    out_ref[2:3, :] = pick(mine & ~direct & (rank_rest == message), pages)
    arrival = pick((tgt_c == own) & (rank_tgt == message), row_c & (ROWS - 1))
    sub16 = lax.broadcasted_iota(jnp.int32, (ROWS, ROWS), 0)
    lane16 = lax.broadcasted_iota(jnp.int32, (ROWS, ROWS), 1)

    def table_column(j):
        spread = jnp.where(sub16 == lane16, table_ref[j : j + 1, :].astype(jnp.float32), 0.0)
        return jnp.sum(spread, axis=1, keepdims=True).astype(jnp.int32)

    table = by_page([table_column(j) for j in range(MAXP)])
    row_id = lax.broadcasted_iota(jnp.int32, (ROWS, WIDTH), 0)
    out_ref[3:4, :] = pick(row_id == arrival, table)
    out_ref[4:5, :] = pick(mine & direct & (rank_out == message), pages)
    out_ref[5:6, :] = arrival
    branch_ref[0] = branch[0, 0]
    out_ref[6:7, :] = pick((tgt_c == own) & ((row_c & (ROWS - 1)) == col), rank_tgt + 1) - 1
    out_ref[7:8, :] = jnp.zeros((1, WIDTH), jnp.int32)


def make_plan(own, mig_row, mig_source, mig_pages, page_table):
    return pl.pallas_call(
        plan_kernel,
        out_shape=(
            jax.ShapeDtypeStruct((8, WIDTH), jnp.int32),
            jax.ShapeDtypeStruct((1,), jnp.int32),
        ),
        in_specs=[spec(SMEM), spec(VMEM), spec(VMEM), spec(VMEM), spec(VMEM)],
        out_specs=(spec(VMEM), spec(SMEM)),
        compiler_params=ALONE,
        cost_estimate=cost(100_000),
    )(own, mig_row, mig_source, mig_pages.T, page_table.T)


def pack_kernel(own_ref, q_ref, k_ref, v_ref, after_ref, *refs):
    blocks, scratch = refs[:TP], refs[TP]
    scratch[...] = jnp.zeros_like(scratch)
    place = own_ref[0] & (TP - 1)

    @pl.loop(0, TP)
    def _(k):
        d = place ^ k
        own_head = pl.ds(pl.multiple_of(d * HD, HD), HD)
        for r in range(2):
            for g in range(GROUP):
                head = pl.ds(pl.multiple_of((d * GROUP + g) * HD, HD), HD)
                scratch[k, r, 2 * g : 2 * g + 2, :] = q_ref[r, :, head].astype(jnp.float32)
            scratch[k, r, 16:18, :] = k_ref[r, :, own_head].astype(jnp.float32)
            scratch[k, r, 18:20, :] = v_ref[r, :, own_head].astype(jnp.float32)

    for k in range(TP):
        blocks[k][...] = scratch[k].astype(jnp.bfloat16)


def pack(own, new_queries, new_keys, new_values, after):
    return pl.pallas_call(
        pack_kernel,
        out_shape=(jax.ShapeDtypeStruct((2, QKV, HD), jnp.bfloat16),) * TP,
        in_specs=[spec(SMEM)] + [spec(VMEM)] * 3 + [spec(pl.ANY)],
        out_specs=(spec(VMEM),) * TP,
        scratch_shapes=[pltpu.VMEM((TP, 2, QKV, HD), jnp.float32)],
        compiler_params=LIMIT,
        cost_estimate=cost(400_000),
    )(own, new_queries, new_keys, new_values, after)


def send_kernel(slots, plan_ref, keys_ref, values_ref, whole_ref, out_ref, held, in_sem, out_sem):
    def load(row, messages, target, j, sem):
        for m in range(messages):
            for part, pool in enumerate((keys_ref, values_ref)):
                source = pool.at[plan_ref[row, m * MAXP + j]]
                slot = target.at[pl.ds(MAXP * j, MAXP), m, part]
                pltpu.make_async_copy(source, slot, sem).start()

    def wait(target, sem):
        pltpu.make_async_copy(target, target, sem).wait()

    for j in range(MAXP):
        load(4, WHOLE, whole_ref, j, in_sem.at[MAXP])
    for j in range(MAXP):
        load(2, slots, held, j, in_sem.at[j])
    sends = []
    for j in range(MAXP):
        block = pl.ds(MAXP * j, MAXP)
        wait(held.at[block], in_sem.at[j])
        send = pltpu.make_async_copy(held.at[block], out_ref.at[block], out_sem.at[j])
        send.start()
        sends.append(send)
    wait(whole_ref, in_sem.at[MAXP])
    for send in sends:
        send.wait()


def outgoing(plan, keys, values, slots):
    held = (SPREAD, slots, 2, PR, HD)
    return pl.pallas_call(
        functools.partial(send_kernel, slots),
        out_shape=(
            jax.ShapeDtypeStruct((SPREAD, WHOLE, 2, PR, HD), jnp.bfloat16),
            jax.ShapeDtypeStruct(held, jnp.bfloat16),
        ),
        in_specs=[spec(SMEM)] + [spec(pl.ANY)] * 2,
        out_specs=(spec(VMEM), spec(HBM)),
        scratch_shapes=[
            pltpu.VMEM(held, jnp.bfloat16),
            pltpu.SemaphoreType.DMA((MAXP + 1,)),
            pltpu.SemaphoreType.DMA((MAXP,)),
        ],
        compiler_params=ROOM,
        cost_estimate=cost(6_000_000),
    )(plan, *(pool.reshape(POOL, MAXP, PR, HD) for pool in (keys, values)))


def touch_kernel(*refs):
    refs[-1][...] = jnp.zeros_like(refs[-1])


def touch(array, *through):
    kept = [jax.ShapeDtypeStruct(a.shape, a.dtype) for a in through]
    return pl.pallas_call(
        touch_kernel,
        out_shape=tuple(kept) + (jax.ShapeDtypeStruct((8, HD), jnp.float32),),
        in_specs=[spec(pl.ANY)] * (1 + len(kept)),
        out_specs=(spec(pl.ANY),) * len(kept) + (spec(VMEM),),
        input_output_aliases={1 + i: i for i in range(len(kept))},
        cost_estimate=cost(FILLER),
    )(array, *through)


def cross_kernel(cap, plan_ref, held_ref, *refs):
    keys_ref, values_ref = refs[-2:]

    @pl.loop(0, cap, step=4)
    def _(base):
        for i in range(4):
            place = plan_ref[0, base + i]
            keys_ref[base + i] = held_ref[place, 0]
            values_ref[base + i] = held_ref[place, 1]


def crossing(plan, held, cap, through, after):
    piece = jax.ShapeDtypeStruct((cap, PR, HD), jnp.bfloat16)
    return pl.pallas_call(
        functools.partial(cross_kernel, cap),
        out_shape=(jax.ShapeDtypeStruct(through.shape, through.dtype), piece, piece),
        in_specs=[spec(SMEM), spec(VMEM), spec(pl.ANY), spec(pl.ANY)],
        out_specs=(spec(pl.ANY), spec(VMEM), spec(VMEM)),
        input_output_aliases={2: 0},
        compiler_params=ALONE,
        cost_estimate=cost(4_000_000),
    )(plan, held, through, after)


def deliver_kernel(slots, part, unread, plan_ref, rest_ref, direct_ref, later_ref, *refs):
    gathered, ordered, in_sem, out_sem = refs[-4:]
    out_ref = refs[unread]
    if part:
        refs[unread + 1][...] = jnp.zeros_like(refs[unread + 1])
    kept = SPREAD * slots
    crossed = kept + SPREAD * WHOLE
    moves = [
        (rest_ref.at[:, part], gathered.at[0:kept]),
        (direct_ref.at[:, part], gathered.at[kept:crossed]),
        (later_ref, gathered.at[crossed:]),
    ]
    copies = [pltpu.make_async_copy(a, b, in_sem.at[i]) for i, (a, b) in enumerate(moves)]
    for copy in copies:
        copy.start()
    for copy in copies:
        copy.wait()
    step = PIECES // 4
    sends = []
    for quarter in range(4):
        first = quarter * step

        @pl.loop(first, first + step, step=11)
        def _(base):
            for i in range(11):
                ordered[base + i] = gathered[plan_ref[1, base + i]]

        block = pl.ds(first, step)
        send = pltpu.make_async_copy(ordered.at[block], out_ref.at[block], out_sem.at[quarter])
        send.start()
        sends.append(send)
    for send in sends:
        send.wait()


def deliver(plan, rest, direct, later, part, beside, *after):
    slots, cap = rest.shape[0] // SPREAD, later.shape[0]
    shapes = (
        jax.ShapeDtypeStruct((PIECES, PR, HD), jnp.bfloat16),
        jax.ShapeDtypeStruct((8, HD), jnp.float32),
    )
    return pl.pallas_call(
        functools.partial(deliver_kernel, slots, part, len(after)),
        out_shape=shapes if part else shapes[0],
        in_specs=[spec(SMEM)] + [spec(pl.ANY)] * (3 + len(after)),
        out_specs=(spec(HBM), spec(VMEM)) if part else spec(HBM),
        scratch_shapes=[
            pltpu.VMEM((SPREAD * (slots + WHOLE) + cap, PR, HD), jnp.bfloat16),
            pltpu.VMEM((PIECES, PR, HD), jnp.bfloat16),
            pltpu.SemaphoreType.DMA((3,)),
            pltpu.SemaphoreType.DMA((4,)),
        ],
        compiler_params=ALONE,
        cost_estimate=cost(beside),
    )(plan, rest, direct, later, *after)


def place_pages(plan_ref, received_ref, moved):
    @pl.loop(0, MOVES)
    def _(k):
        for j in range(MAXP):
            page = plan_ref[3, k * MAXP + j]
            for quarter in range(MAXP):
                first = quarter * PR
                moved[page, first : first + PR, :] = received_ref[MAXP * j + quarter, k]


def keys_kernel(own_ref, plan_ref, table_ref, lengths_ref, pool_ref, received_ref, values_ref, *refs):
    blocks, (out_ref, cache_ref, known_ref, moved_ref, sem, qkv, scores, fresh_scores) = refs[:TP], refs[TP:]
    load = pltpu.make_async_copy(pool_ref, moved_ref, sem.at[0])
    store = pltpu.make_async_copy(moved_ref, out_ref, sem.at[1])
    load.start()
    scale = 1.0 / math.sqrt(HD)
    position = lax.broadcasted_iota(jnp.int32, (16, PAGE), 1)
    fresh_index = lax.broadcasted_iota(jnp.int32, (16, 16), 1)
    step = lax.broadcasted_iota(jnp.int32, (16, 16), 0) & 1
    by_rows = (((1,), (1,)), ((), ()))
    first_row = (own_ref[0] >> 3) * ROWS
    place = own_ref[0] & (TP - 1)
    for k in range(TP):
        qkv[pl.ds((place ^ k) * 2, 2)] = blocks[k][...]
    load.wait()
    place_pages(plan_ref, received_ref, moved_ref)
    store.start()

    @pl.loop(0, ROWS, step=4)
    def _(base):
        for i in range(4):
            r = base + i
            queries = qkv[r, 0:16, :]
            length = lengths_ref[first_row + r]
            for j in range(MAXP):
                page = moved_ref[table_ref[j, r]]
                part = lax.dot_general(queries, page, by_rows, preferred_element_type=jnp.float32)
                part = jnp.where(position + j * PAGE < length, part * scale, -jnp.inf)
                scores[r, :, j * PAGE : (j + 1) * PAGE] = part
            part = lax.dot_general(
                queries, qkv[r, 16:32, :], by_rows, preferred_element_type=jnp.float32
            )
            fresh_scores[r] = jnp.where(fresh_index <= step, part * scale, -jnp.inf)

    @pl.loop(0, ROWS, step=4)
    def _(base):
        rows = pl.ds(base, 4)
        cache, fresh = scores[rows], fresh_scores[rows]
        top = jnp.maximum(
            jnp.max(cache, axis=-1, keepdims=True), jnp.max(fresh, axis=-1, keepdims=True)
        )
        cache, fresh = jnp.exp(cache - top), jnp.exp(fresh - top)
        total = jnp.sum(cache, axis=-1, keepdims=True) + jnp.sum(fresh, axis=-1, keepdims=True)
        cache_ref[rows] = (cache / total).astype(jnp.bfloat16)
        fresh = (fresh / total).astype(jnp.bfloat16).astype(jnp.float32)
        values = qkv[rows, 16:32, :].astype(jnp.float32)
        known_ref[rows] = fresh[:, :, 0:1] * values[:, 2:3, :] + fresh[:, :, 1:2] * values[:, 3:4, :]

    @pl.loop(0, ROWS)
    def _(r):
        @pl.when(plan_ref[6, r] < 0)
        def _():
            cached = jnp.zeros((16, HD), jnp.float32)
            for j in range(MAXP):
                weights = cache_ref[r, :, j * PAGE : (j + 1) * PAGE]
                page = values_ref[table_ref[j, r]]
                cached += jnp.dot(weights, page, preferred_element_type=jnp.float32)
            known_ref[r] += cached

    store.wait()


def keys_step(own, plan, table, lengths, pool, received, values, blocks):
    return pl.pallas_call(
        keys_kernel,
        out_shape=(
            jax.ShapeDtypeStruct((POOL, PAGE, HD), jnp.bfloat16),
            jax.ShapeDtypeStruct((ROWS, 16, MAXP * PAGE), jnp.bfloat16),
            jax.ShapeDtypeStruct((ROWS, 16, HD), jnp.float32),
        ),
        in_specs=[spec(SMEM)] * 4 + [spec(pl.ANY)] + [spec(VMEM)] * (2 + TP),
        out_specs=(spec(pl.ANY), spec(VMEM), spec(VMEM)),
        scratch_shapes=[
            pltpu.VMEM((POOL, PAGE, HD), jnp.bfloat16),
            pltpu.SemaphoreType.DMA((2,)),
            pltpu.VMEM((ROWS, QKV, HD), jnp.bfloat16),
            pltpu.VMEM((ROWS, 16, MAXP * PAGE), jnp.float32),
            pltpu.VMEM((ROWS, 16, 16), jnp.float32),
        ],
        compiler_params=LIMIT,
        cost_estimate=cost(8_000_000),
    )(own, plan, table, lengths, pool, received, values, *blocks)


def values_kernel(plan_ref, cache_ref, known_ref, received_ref, out_ref, mixed):
    mixed[...] = known_ref[...]
    for k in range(MOVES):
        r = plan_ref[5, k * MAXP]
        values = received_ref[:, k].reshape(MAXP * PAGE, HD)
        mixed[r] = known_ref[r] + jnp.dot(
            cache_ref[r], values, preferred_element_type=jnp.float32
        )
    for r in range(ROWS):
        row = mixed[r]
        for g in range(GROUP):
            head = row[2 * g : 2 * g + 2, :].astype(jnp.bfloat16)
            out_ref[r, :, g * HD : (g + 1) * HD] = head


def values_step(plan, weights, known, received):
    return pl.pallas_call(
        values_kernel,
        out_shape=jax.ShapeDtypeStruct((ROWS, 2, GROUP * HD), jnp.bfloat16),
        in_specs=[spec(SMEM)] + [spec(VMEM)] * 3,
        out_specs=spec(VMEM),
        scratch_shapes=[pltpu.VMEM((ROWS, 16, HD), jnp.float32)],
        compiler_params=LIMIT,
        cost_estimate=cost(4_000_000),
    )(plan, weights, known, received)


def place_kernel(plan_ref, pool_ref, received_ref, out_ref, moved, arrived, sem):
    pairs = [(pool_ref, moved), (received_ref, arrived)]
    loads = [pltpu.make_async_copy(a, b, sem.at[i]) for i, (a, b) in enumerate(pairs)]
    store = pltpu.make_async_copy(moved, out_ref, sem.at[2])
    for load in loads:
        load.start()
    for load in loads:
        load.wait()
    place_pages(plan_ref, arrived, moved)
    store.start()
    store.wait()


def place_step(plan, pool, received):
    return pl.pallas_call(
        place_kernel,
        out_shape=jax.ShapeDtypeStruct((POOL, PAGE, HD), jnp.bfloat16),
        in_specs=[spec(SMEM), spec(pl.ANY), spec(pl.ANY)],
        out_specs=spec(pl.ANY),
        scratch_shapes=[
            pltpu.VMEM((POOL, PAGE, HD), jnp.bfloat16),
            pltpu.VMEM((SPREAD, MOVES, PR, HD), jnp.bfloat16),
            pltpu.SemaphoreType.DMA((3,)),
        ],
        compiler_params=LIMIT,
        cost_estimate=cost(8_000_000),
    )(plan, pool, received)


def swap(array, axes):
    return lax.all_to_all(array, axes, split_axis=0, concat_axis=0, tiled=True)


def cross(array):
    return lax.ppermute(array, "zh", [(0, 1), (1, 0)])


def move_and_attend(
    slots, cap, own, plan, table, lengths, new_queries, new_keys, new_values, key_pool, value_pool
):
    direct, send = outgoing(plan, key_pool, value_pool, slots)
    direct = cross(direct)
    held = swap(send, ("y", "x")).reshape(SPREAD * slots, 2, PR, HD)
    direct, leaving_keys, leaving_values = crossing(plan, held, cap, direct, *touch(direct))
    later_keys = cross(leaving_keys)
    leaving_values, token = touch(later_keys, leaving_values)
    later_values = cross(leaving_values)
    direct = swap(direct, ("y", "x")).reshape(SPREAD * WHOLE, 2, PR, HD)
    final_keys = deliver(plan, held, direct, later_keys, 0, 4_000_000, token)
    received_keys = swap(final_keys.reshape(SPREAD, MOVES, PR, HD), ("y", "x"))
    final_values, token = deliver(plan, held, direct, later_values, 1, FILLER)
    blocks = list(pack(own, new_queries, new_keys, new_values, token))
    for k in range(1, TP):
        blocks[k] = lax.ppermute(blocks[k], ("zl", "c"), [(i, i ^ k) for i in range(TP)])
    received_values = swap(final_values.reshape(SPREAD, MOVES, PR, HD), ("y", "x"))
    key_moved, weights, known = keys_step(
        own, plan, table, lengths, key_pool, received_keys, value_pool, blocks
    )
    return key_moved, weights, known, received_values


def body(
    new_queries,
    new_keys,
    new_values,
    key_pool,
    value_pool,
    lengths,
    page_table,
    mig_row,
    mig_source,
    mig_pages,
):
    own = lax.axis_index(("y", "zh", "x", "zl", "c")).astype(jnp.int32).reshape(1)
    plan, branch = make_plan(own, mig_row, mig_source, mig_pages, page_table)
    key_moved, weights, known, received_values = lax.switch(
        branch[0],
        [functools.partial(move_and_attend, slots, cap) for slots, cap in BRANCHES],
        own,
        plan,
        page_table.T,
        lengths,
        new_queries,
        new_keys,
        new_values,
        key_pool,
        value_pool,
    )
    mixed = values_step(plan, weights, known, received_values)
    attention = lax.all_to_all(mixed, ("zl", "c"), split_axis=0, concat_axis=2, tiled=True)
    value_moved = place_step(plan, value_pool, received_values)
    return (attention, key_moved, value_moved)


def solution(mesh):
    fine = Mesh(mesh.devices.reshape(4, NZ, NX, 4, 2), ("y", "zh", "x", "zl", "c"))
    inst, tp = ("y", "zh", "x"), ("zl", "c")
    rows = P(inst + tp, None, None)
    pool = P(inst, None, tp)
    return jax.shard_map(
        body,
        mesh=fine,
        in_specs=(rows, rows, rows, pool, pool, P(), P(inst, None), P(), P(), P()),
        out_specs=(rows, pool, pool),
        check_vma=False,
    )
```
